512 devices in a mesh: dp: 16 (over y, core), proto: 32 (over z, x).
Axes of the slice: x: 4, y: 8, z: 8, core: 2. Of those that a mesh axis runs over, the one named last changes fastest.
Arguments:
- teacher_feat: bfloat16 [6144, 384], P('dp'), may hold values from -3 to 3
- student_feat: bfloat16 [6144, 384], P('dp'), may hold values from -3 to 3
- prototypes: bfloat16 [131072, 384], P('proto'), may hold values from -3 to 3
- row_weight: float32 [6144], P('dp'), may hold values from 200 to 2000
Outputs:
- row_loss: float32 [6144], P('dp')
- grad_student: float32 [6144, 384], P(('dp', 'proto'))
- grad_proto: bfloat16 [131072, 384], P(('proto', 'dp'))
The draws below stay inside these ranges and needn't reach their ends.
All inputs are finite; a program needn't handle non-finite values.
Results may differ from the reference program's by a relative error of at most 0.03.
Values may be sent and summed in bfloat16 or wider, within the bound.
A program may use at most 64 MiB of HBM per device.

```python
import math
import jax
import jax.numpy as jnp
from jax import lax

D = 384
PROTOS = 131072
ROWS = 384
ITERS = 3
ALL_ROWS = 6144
N_DP = 16
N_PROTO = 32


def shared_parts(key):
    groups = max(PROTOS // 256, 16)
    perm_key, ceiling_key, ranking_key, centre_key = jax.random.split(key, 4)
    ordering = jax.random.permutation(perm_key, groups)
    ceiling = jax.random.randint(ceiling_key, (ALL_ROWS,), 1, groups + 1)
    ranking = jax.random.randint(ranking_key, (ALL_ROWS,), 0, ceiling)
    members = ordering[ranking]
    centres = jax.random.normal(centre_key, (groups, D), jnp.float32)
    return (members, centres)


def blend(centre_rows, noise, share):
    mixed = jnp.sqrt(share) * centre_rows + jnp.sqrt(1.0 - share) * noise
    return jnp.clip(mixed, -3.0, 3.0)


def draw_teacher_feat(key, part):
    members, centres = shared_parts(key)
    key = jax.random.fold_in(key, 11)
    share_key, noise_key = jax.random.split(key)
    noise = jax.random.normal(noise_key, (ALL_ROWS, D), jnp.float32)
    share = jax.random.uniform(share_key, (ALL_ROWS, 1), jnp.float32, 0.35, 0.65)
    return blend(centres[members], noise, share).astype(jnp.bfloat16)


def draw_student_feat(key, part):
    members, centres = shared_parts(key)
    key = jax.random.fold_in(key, 12)
    share_key, noise_key = jax.random.split(key)
    noise = jax.random.normal(noise_key, (ALL_ROWS, D), jnp.float32)
    share = jax.random.uniform(share_key, (ALL_ROWS, 1), jnp.float32, 0.35, 0.65)
    return blend(centres[members], noise, share).astype(jnp.bfloat16)


def draw_prototypes(key, part):
    members, centres = shared_parts(key)
    key = jax.random.fold_in(key, 13)
    share_key, noise_key = jax.random.split(key)
    groups = max(PROTOS // 256, 16)
    owners = jnp.arange(PROTOS, dtype=jnp.int32) // (PROTOS // groups)
    noise = jax.random.normal(noise_key, (PROTOS, D), jnp.float32)
    share = jax.random.uniform(share_key, (PROTOS, 1), jnp.float32, 0.3, 0.7)
    return blend(centres[owners], noise, share).astype(jnp.bfloat16)


def block_levels(own_key, extent, shards, smallest, top_value):
    def one(dim, shards_of):
        heights = jax.random.uniform(jax.random.fold_in(jax.random.fold_in(own_key, 6), dim), (shards_of,), jnp.float32, smallest / len(shards), top_value / len(shards))
        return jnp.repeat(jnp.exp(heights), extent[dim] // shards_of).reshape((-1,) + (1,) * (len(extent) - dim - 1))

    level = one(*shards[0])
    for cut in shards[1:]:
        level = level * one(*cut)
    return level


def setup_inputs(seed: int = 0) -> dict:
    key_of = jax.random.split(jax.random.key(seed), 5)
    teacher_feat = draw_teacher_feat(jax.random.fold_in(key_of[4], 71), 0)
    student_feat = draw_student_feat(jax.random.fold_in(key_of[4], 71), 0)
    prototypes = draw_prototypes(jax.random.fold_in(key_of[4], 71), 0)
    row_weight = jnp.clip(jnp.exp(math.log(2000.0) - 2.3025851 * jax.random.uniform(key_of[3], (ALL_ROWS,), jnp.float32) ** block_levels(key_of[3], (ALL_ROWS,), ((0, 16),), -0.2, 0.2)), 200.0, 2000.0)
    return dict(teacher_feat=teacher_feat, student_feat=student_feat, prototypes=prototypes, row_weight=row_weight)


teacher_temp = 0.04
student_temp = 0.1
norm_eps = 1e-06

def normalize_rows(values):
    floats = values.astype(jnp.float32)
    length = jnp.sqrt(lax.optimization_barrier(jnp.sum(floats * floats, axis=-1, keepdims=True)) + norm_eps)
    return (floats / length, length)

def reference(teacher_feat, student_feat, prototypes, row_weight):
    tunit, tlength = normalize_rows(teacher_feat)
    tn = tunit.astype(jnp.bfloat16)
    sunit, snorm = normalize_rows(student_feat)
    sn = sunit.astype(jnp.bfloat16)
    width = PROTOS // N_PROTO
    blocks = prototypes.reshape(N_PROTO, width, D)
    all_rows = ROWS * N_DP

    def block_parts(block):
        wunit, wnorm = normalize_rows(block)
        wn = wunit.astype(jnp.bfloat16)
        expo = jnp.exp(jnp.dot(tn, wn.T, preferred_element_type=jnp.float32) / teacher_temp)
        return (wunit, wnorm, wn, expo)
    rowscale = jnp.ones((all_rows,), jnp.float32)
    colscales = jnp.zeros((N_PROTO, width), jnp.float32)
    for step in range(ITERS):

        def col_block(block):
            expo = block_parts(block)[3]
            return 1.0 / lax.optimization_barrier(jnp.sum(expo * rowscale[:, None], axis=0))
        colscales = lax.map(col_block, blocks)

        def row_block(total, inputs):
            block, colscale = inputs
            expo = block_parts(block)[3]
            return (total + lax.optimization_barrier(jnp.sum(expo * colscale[None, :], axis=1)), None)
        totals, unused = lax.scan(row_block, jnp.zeros((all_rows,), jnp.float32), (blocks, colscales))
        rowscale = 1.0 / totals

    def stat_block(carry, inputs):
        block, colscale = inputs
        parts = block_parts(block)
        scores = jnp.dot(sn, parts[2].T, preferred_element_type=jnp.float32) / student_temp
        expsum = carry[0] + lax.optimization_barrier(jnp.sum(jnp.exp(scores), axis=1))
        weighted = carry[1] + lax.optimization_barrier(jnp.sum(parts[3] * colscale[None, :] * scores, axis=1))
        return ((expsum, weighted), None)
    zeros_rows = jnp.zeros((all_rows,), jnp.float32)
    (expsum, qz_pre), unused = lax.scan(stat_block, (zeros_rows, zeros_rows), (blocks, colscales))
    lse = jnp.log(expsum)
    row_loss = lse - rowscale * qz_pre

    def grad_block(dsn, inputs):
        block, colscale = inputs
        wunit, wnorm, wn, expo = block_parts(block)
        scores = jnp.dot(sn, wn.T, preferred_element_type=jnp.float32) / student_temp
        probs = jnp.exp(scores - lse[:, None])
        target = expo * colscale[None, :] * rowscale[:, None]
        dscore = (row_weight[:, None] * (probs - target) / student_temp).astype(jnp.bfloat16)
        xg = jnp.einsum('gik,gid->gkd', dscore.reshape(N_DP, ROWS, width).astype(jnp.float32), sn.reshape(N_DP, ROWS, D).astype(jnp.float32))
        terms = (xg - wunit[None] * lax.optimization_barrier(jnp.sum(wunit[None] * xg, axis=-1, keepdims=True))) / wnorm[None]
        rounded = lax.optimization_barrier(terms.astype(jnp.bfloat16)).astype(jnp.float32)
        gblock = lax.optimization_barrier(jnp.sum(rounded, axis=0)).astype(jnp.bfloat16)
        dsn = dsn + jnp.dot(dscore, wn, preferred_element_type=jnp.float32)
        return (dsn, gblock)
    dsn, gblocks = lax.scan(grad_block, jnp.zeros((all_rows, D), jnp.float32), (blocks, colscales))
    grad_proto = gblocks.reshape(PROTOS, D)
    grad_student = (dsn - sunit * lax.optimization_barrier(jnp.sum(sunit * dsn, axis=1, keepdims=True))) / snorm
    return (row_loss, grad_student, grad_proto)
```

```python
import jax
import jax.numpy as jnp
from jax import lax
from jax.experimental import pallas as pl
from jax.experimental.pallas import tpu as pltpu
from jax.sharding import PartitionSpec as P

MESH = pl.DeviceIdType.MESH
F32, BF16 = jnp.float32, jnp.bfloat16
ITERS = 3
NY, NC, NZ, NX = 8, 2, 8, 4
NP = NZ * NX
R = 384
D = 384
KB = 256
NB = 8
ZR = R // NZ
PR = R // NP
EPS = 1e-6
NT = (((1,), (1,)), ((), ()))


def hops(step, size):
    return min(step, size - step)


Y_STEPS = sorted(range(1, NY), key=lambda a: -hops(a, NY))
Z_STEPS = sorted(range(1, NZ), key=lambda a: -hops(a, NZ))
X_STEPS = sorted(range(1, NX), key=lambda a: -hops(a, NX))
ZX_STEPS = sorted(
    [(a, b) for a in range(NZ) for b in range(NX) if (a, b) != (0, 0)],
    key=lambda s: -(hops(s[0], NZ) + hops(s[1], NX)),
)


def unit_rows(values):
    floats = values.astype(F32)
    return floats * lax.rsqrt(jnp.sum(floats * floats, axis=-1, keepdims=True) + EPS)


def two_rows(vector):
    high = vector.astype(BF16).astype(F32)
    low = vector - high
    rows = lax.broadcasted_iota(jnp.int32, (16, vector.shape[1]), 0)
    return jnp.where(rows == 0, high, jnp.where(rows == 1, low, 0.0)).astype(BF16)


def pack(vectors, rows):
    parts = [v[:, j : j + 128] for v in vectors for j in range(0, v.shape[1], 128)]
    if len(parts) < rows:
        parts.append(jnp.zeros((rows - len(parts), 128), F32))
    return jnp.concatenate(parts, axis=0)


def unpack(tile, start, count):
    return jnp.concatenate([tile[j : j + 1, :] for j in range(start, start + count)], axis=1)


def kernel(
    t_ref, s_ref, w_ref, rw_ref, loss_ref, gs_ref, gp_ref,
    wraw, wfraw, wn, wnt, wnf, tn2, sn2, gt, gs, snt, expo, expoz, prob, ef, pf, uw,
    vacc, scaled, cvec, ybuf, zxbuf, cbuf, c3buf, auxc, auxzx, abuf, bbuf,
    ucs, ucr, uzs, uzr, uxs, uxr, vsend, vrecv, bsend, brecv,
    wsem, xs, xr, ys, yr, zxs, zxr, cs, cr, gts, gtr, tcs, tcr, scs, scr, abs_, abr,
    us, ur, vbs, vbr,
):
    dp, pr = lax.axis_index("dp"), lax.axis_index("proto")
    y, c = lax.div(dp, NC), lax.rem(dp, NC)
    z, x = lax.div(pr, NX), lax.rem(pr, NX)
    o = 1 - c

    def dev(yy, cc, zz, xx):
        return {"dp": yy * NC + cc, "proto": zz * NX + xx}

    sibling = dev(y, o, z, x)
    y_at = lambda a: lax.rem(y + a, NY)
    z_at = lambda a: lax.rem(z + a, NZ)
    x_at = lambda a: lax.rem(x + a, NX)
    late = []

    def wait_for(ref, sem):
        pltpu.make_async_copy(ref, ref, sem).wait()

    def send(src, dst, ss, rs, to):
        pltpu.make_async_remote_copy(
            src_ref=src, dst_ref=dst, send_sem=ss, recv_sem=rs, device_id=to, device_id_type=MESH
        ).start()

    def send_y(ref, ss, rs):
        for a in Y_STEPS:
            send(ref.at[y], ref.at[y], ss, rs, dev(y_at(a), c, z, x))
        late.append((ref.at[pl.ds(0, NY - 1)], ss))

    def send_zx(ref, ss, rs):
        for a, b in ZX_STEPS:
            send(ref.at[pr], ref.at[pr], ss, rs, dev(y, c, z_at(a), x_at(b)))
        late.append((ref.at[pl.ds(0, NP - 1)], ss))

    def send_core(src, dst, ss, rs):
        send(src, dst, ss, rs, sibling)
        late.append((src, ss))

    loads = [
        pltpu.make_async_copy(w_ref.at[pl.ds((2 * b + c) * KB, KB)], wraw.at[b], wsem.at[b])
        for b in range(NB)
    ]
    loads.append(pltpu.make_async_copy(w_ref.at[pl.ds(2 * y * KB, 2 * KB)], wfraw, wsem.at[NB]))
    for load in loads:
        load.start()
    barrier = pltpu.get_barrier_semaphore()
    peers = [sibling]
    peers += [dev(y, c, z_at(a), x_at(b)) for a, b in ZX_STEPS]
    peers += [dev(y_at(a), c, z, x) for a in Y_STEPS]
    for peer in peers:
        pl.semaphore_signal(barrier, inc=1, device_id=peer, device_id_type=MESH)

    tn2[c] = unit_rows(t_ref[...]).astype(BF16)
    sn_own = unit_rows(s_ref[...]).astype(BF16)
    sn2[c] = sn_own
    gs[y] = sn_own
    gt[z, y] = tn2[c, pl.ds(pl.multiple_of(z * ZR, 16), ZR), :]
    for load in loads:
        load.wait()

    def norm_block(b, carry):
        block = unit_rows(wraw[b]).astype(BF16)
        wn[b] = block
        wnt[b] = block.T
        return carry

    lax.fori_loop(0, NB, norm_block, 0)
    for h in range(NC):
        wnf[h] = unit_rows(wfraw[pl.ds(h * KB, KB), :]).astype(BF16)

    def score_rows(h, first):
        def block(b, carry):
            w = wn[b]
            st = lax.dot_general(tn2[h], w, NT, preferred_element_type=F32)
            e = jnp.exp(st * 25.0)
            zs = lax.dot_general(sn2[h], w, NT, preferred_element_type=F32) * 10.0
            expo[b, h] = e.astype(BF16)
            expoz[b, h] = (e * zs).astype(BF16)
            prob[b, h] = jnp.exp(zs).astype(BF16)
            total = jnp.sum(e, axis=0, keepdims=True)
            if not first:
                total = total + ybuf[0, y, pl.ds(b, 1), :]
            ybuf[0, y, pl.ds(b, 1), :] = total
            return carry

        lax.fori_loop(0, NB, block, 0)

    score_rows(c, True)

    pl.semaphore_wait(barrier, len(peers))
    send_core(tn2.at[c], tn2.at[c], xs.at[0], xr.at[0])
    send_core(sn2.at[c], sn2.at[c], xs.at[1], xr.at[1])
    for a in Y_STEPS:
        send(gt.at[z, y], gt.at[z, y], gts.at[0], gtr.at[0], dev(y_at(a), c, z, x))
    late.append((gt.at[0, pl.ds(0, NY - 1)], gts.at[0]))

    def y_chain(step):
        if step > 1:
            for way, back in ((0, -(step - 1)), (1, step - 1)):
                wait_for(gs.at[y_at(NY + back)], scr.at[way, step - 2])
        for way, back, to in ((0, -(step - 1), 1), (1, step - 1, -1)):
            src = gs.at[y_at(NY + back)]
            if step == 4:
                src = src.at[pl.ds(way * (R // 2), R // 2)]
            send(src, src, scs.at[way, step - 1], scr.at[way, step - 1], dev(y_at(NY + to), c, z, x))
            late.append((src, scs.at[way, step - 1]))

    def y_chain_end():
        for way in range(2):
            wait_for(gs.at[y_at(4), pl.ds(way * (R // 2), R // 2)], scr.at[way, 3])

    def z_chain(step):
        if step == 1:
            wait_for(gt.at[z, pl.ds(0, NY - 1)], gtr.at[0])
        else:
            for way, back in ((0, -(step - 1)), (1, step - 1)):
                wait_for(gt.at[z_at(NZ + back)], tcr.at[way, step - 2])
        for way, back, to in ((0, -(step - 1), 1), (1, step - 1, -1)):
            src = gt.at[z_at(NZ + back)]
            if step == 4:
                src = src.at[pl.ds(way * (NY // 2), NY // 2)]
            send(src, src, tcs.at[way, step - 1], tcr.at[way, step - 1], dev(y, c, z_at(NZ + to), x))
            late.append((src, tcs.at[way, step - 1]))

    def z_chain_end():
        for way in range(2):
            wait_for(gt.at[z_at(4), pl.ds(way * (NY // 2), NY // 2)], tcr.at[way, 3])

    def fill_teacher(slice_):
        rows = gt[slice_].reshape(R, D)
        for h in range(NC):
            st = lax.dot_general(rows, wnf[h], NT, preferred_element_type=F32)
            e = jnp.exp(st * 25.0).astype(BF16)
            for g in range(NY):
                ef[h, g, slice_] = e[g * ZR : (g + 1) * ZR]

    def fill_student(group):
        rows = gs[group]
        snt[group] = rows.T
        for h in range(NC):
            zs = lax.dot_general(rows, wnf[h], NT, preferred_element_type=F32) * 10.0
            pf[group, h] = jnp.exp(zs).astype(BF16)

    y_chain(1)
    fill_student(y)
    wait_for(tn2.at[o], xr.at[0])
    wait_for(sn2.at[o], xr.at[1])
    score_rows(o, False)

    def own(v):
        return jnp.where(c == 0, v[:, :R], v[:, R:])

    def other(v):
        return jnp.where(c == 0, v[:, R:], v[:, :R])

    def row_sums(lhs, mats):
        sums = [jnp.zeros((16, NC * R), F32) for _ in mats]
        for b in range(NB):
            left = lhs(b)
            for i, mat in enumerate(mats):
                sums[i] = sums[i] + lax.dot_general(
                    left, mat[b].reshape(NC * R, KB), NT, preferred_element_type=F32
                )
        return [s[0:1] + s[1:2] for s in sums]

    def sum_protos(q, mat, scale):
        def half(h, carry):
            left = jnp.concatenate([mat[b, h] for b in range(NB)], axis=1)
            if scale is None:
                right = jnp.concatenate([wnt[b] for b in range(NB)], axis=1)
            else:
                right = jnp.concatenate(
                    [(wnt[b].astype(F32) * scale[b : b + 1, :]).astype(BF16) for b in range(NB)], axis=1
                )
            uw[q, h] = lax.dot_general(left, right, NT, preferred_element_type=F32)
            return carry

        lax.fori_loop(0, NC, half, 0)
        ucs[q] = uw[q, o].astype(BF16)
        send_core(ucs.at[q], ucr.at[q], us.at[q, 0], ur.at[q, 0])

    def student_z(q):
        wait_for(ucr.at[q], ur.at[q, 0])
        total = uw[q, c] + ucr[q].astype(F32)
        uzs[q] = total.astype(BF16).reshape(NZ, ZR, D)
        uzr[q, z] = uzs[q, z]
        for a in Z_STEPS:
            send(uzs.at[q, z_at(a)], uzr.at[q, z], us.at[q, 1], ur.at[q, 1], dev(y, c, z_at(a), x))
        late.append((uzs.at[q, pl.ds(0, NZ - 1)], us.at[q, 1]))

    def student_x(q):
        wait_for(uzr.at[q, pl.ds(0, NZ - 1)], ur.at[q, 1])
        total = jnp.sum(uzr[q].astype(F32), axis=0)
        pad = jnp.zeros((16 - PR, D), F32)
        for i in range(NX):
            uxs[q, i] = jnp.concatenate([total[i * PR : (i + 1) * PR], pad], axis=0).astype(BF16)
        uxr[q, x] = uxs[q, x]
        for a in X_STEPS:
            send(uxs.at[q, x_at(a)], uxr.at[q, x], us.at[q, 2], ur.at[q, 2], dev(y, c, z, x_at(a)))
        late.append((uxs.at[q, pl.ds(0, NX - 1)], us.at[q, 2]))

    def student_end(q):
        wait_for(uxr.at[q, pl.ds(0, NX - 1)], ur.at[q, 2])
        return jnp.sum(uxr[q].astype(F32), axis=0)

    rowscale = None
    for it in range(ITERS):
        last = it == ITERS - 1
        if it > 0:
            left = two_rows(rowscale)
            for b in range(NB):
                both = jnp.dot(left, expo[b].reshape(NC * R, KB), preferred_element_type=F32)
                ybuf[it, y, b : b + 1, :] = both[0:1] + both[1:2]
        send_y(ybuf.at[it], ys.at[it], yr.at[it])
        if it == 0:
            rows16 = lax.broadcasted_iota(jnp.int32, (16, KB), 0)
            ones = jnp.where(rows16 == 0, 1.0, 0.0).astype(BF16)
            (expsum,) = row_sums(lambda b: ones, [prob])
            auxc[0] = pack([other(expsum)], 4)
            send_core(auxc.at[0], auxc.at[1], cs.at[ITERS], cr.at[ITERS])
            expsum_own = own(expsum)
            sum_protos(0, prob, None)
        elif it == 1:
            wait_for(auxc.at[1], cr.at[ITERS])
            auxzx[pr] = pack([expsum_own], 4) + auxc[1]
            send_zx(auxzx, zxs.at[ITERS], zxr.at[ITERS])
            fill_teacher(z)
            z_chain(2)
        else:
            wait_for(auxzx.at[pl.ds(0, NP - 1)], zxr.at[ITERS])
            expsum = unpack(jnp.sum(auxzx[...], axis=0), 0, 3)
            lse = jnp.log(expsum)
            weight = rw_ref[...] * 10.0
            alpha = weight / expsum
            abuf[y] = pack([alpha], 4)
            send_y(abuf, abs_.at[0], abr.at[0])
            z_chain(3)
            fill_teacher(z_at(1))
            fill_teacher(z_at(NZ - 1))
        wait_for(ybuf.at[it, pl.ds(0, NY - 1)], yr.at[it])
        colscale = 1.0 / jnp.sum(ybuf[it], axis=0)
        cvec[...] = colscale
        if not last:
            (tot,) = row_sums(lambda b: two_rows(cvec[b : b + 1, :]), [expo])
            zxbuf[it, pr] = pack([tot], 8)
        else:
            tot, qz = row_sums(lambda b: two_rows(cvec[b : b + 1, :]), [expo, expoz])
            c3buf[0] = pack([other(tot), other(qz)], 8)
            send_core(c3buf.at[0], c3buf.at[1], cs.at[it], cr.at[it])
            mine = pack([own(tot), own(qz)], 8)
            wait_for(c3buf.at[1], cr.at[it])
            zxbuf[it, pr] = mine + c3buf[1]
        send_zx(zxbuf.at[it], zxs.at[it], zxr.at[it])
        if it == 0:
            z_chain(1)
            y_chain(2)
            student_z(0)
        elif it == 1:
            y_chain(3)
            fill_student(y_at(1))
            fill_student(y_at(NY - 1))
            student_x(0)
        else:
            sum_protos(1, expo, colscale)
            y_chain(4)
            z_chain(4)
            fill_student(y_at(2))
            fill_student(y_at(NY - 2))
        wait_for(zxbuf.at[it, pl.ds(0, NP - 1)], zxr.at[it])
        sums = jnp.sum(zxbuf[it], axis=0)
        if not last:
            cbuf[it, c] = sums
            send_core(cbuf.at[it, c], cbuf.at[it, c], cs.at[it], cr.at[it])
            wait_for(cbuf.at[it, o], cr.at[it])
            rowscale = 1.0 / unpack(cbuf[it, 0] + cbuf[it, 1], 0, 6)
    rowscale = 1.0 / unpack(sums, 0, 3)
    loss_ref[...] = lse - rowscale * unpack(sums, 3, 3)
    beta = weight * rowscale
    bbuf[y] = pack([beta], 4)
    send_y(bbuf, abs_.at[1], abr.at[1])

    student_z(1)
    fill_teacher(z_at(2))
    fill_teacher(z_at(NZ - 2))
    fill_teacher(z_at(3))
    fill_teacher(z_at(NZ - 3))
    fill_student(y_at(3))
    fill_student(y_at(NY - 3))
    y_chain_end()
    z_chain_end()
    fill_student(y_at(4))
    fill_teacher(z_at(4))
    wait_for(abuf.at[pl.ds(0, NY - 1)], abr.at[0])

    def scale_students(buf):
        for g in range(NY):
            factor = unpack(buf[g], 0, 3)
            scaled[:, g * R : (g + 1) * R] = (snt[g].astype(F32) * factor).astype(BF16)

    scale_students(abuf)

    def student_part(h):
        right = jnp.concatenate([pf[g, h] for g in range(NY)], axis=0)
        return jnp.dot(scaled[...], right, preferred_element_type=F32)

    def teacher_part(h):
        right = ef[h].reshape(NY * R, KB)
        return jnp.dot(scaled[...], right, preferred_element_type=F32)

    vsend[...] = student_part(o).astype(BF16)
    send_core(vsend, vrecv, vbs.at[0], vbr.at[0])
    vacc[...] = student_part(c)
    student_x(1)
    wait_for(bbuf.at[pl.ds(0, NY - 1)], abr.at[1])
    scale_students(bbuf)
    bsend[...] = teacher_part(o).astype(BF16)
    send_core(bsend, brecv, vbs.at[1], vbr.at[1])
    teacher = teacher_part(c)

    rows = lax.broadcasted_iota(jnp.int32, (16, R), 0)
    lanes = lax.broadcasted_iota(jnp.int32, (16, R), 1)
    pick = jnp.where((lanes == rows + pr * PR) & (rows < PR), 1.0, 0.0)
    dsn = jnp.sum(pick * alpha, axis=1, keepdims=True) * student_end(0)
    dsn = dsn - jnp.sum(pick * beta, axis=1, keepdims=True) * student_end(1)
    mine = jnp.dot(pick.astype(BF16), s_ref[...], preferred_element_type=F32)
    inv = lax.rsqrt(jnp.sum(mine * mine, axis=1, keepdims=True) + EPS)
    mine = mine * inv
    grad = (dsn - mine * jnp.sum(mine * dsn, axis=1, keepdims=True)) * inv
    gs_ref[...] = grad[:PR]

    wait_for(vrecv, vbr.at[0])
    wait_for(brecv, vbr.at[1])
    xg = vacc[...] + vrecv[...].astype(F32) - cvec[pl.ds(y, 1), :] * (teacher + brecv[...].astype(F32))
    xg = xg.T
    floats = wraw[y].astype(F32)
    inv = lax.rsqrt(jnp.sum(floats * floats, axis=1, keepdims=True) + EPS)
    unit = floats * inv
    gp_ref[...] = ((xg - unit * jnp.sum(unit * xg, axis=1, keepdims=True)) * inv).astype(BF16)

    for ref, sem in late:
        wait_for(ref, sem)


def shards(teacher_feat, student_feat, prototypes, row_weight):
    vmem = pl.BlockSpec(memory_space=pltpu.VMEM)
    dma = pltpu.SemaphoreType.DMA
    scratch = [
        pltpu.VMEM((NB, KB, D), BF16),
        pltpu.VMEM((2 * KB, D), BF16),
        pltpu.VMEM((NB, KB, D), BF16),
        pltpu.VMEM((NB, D, KB), BF16),
        pltpu.VMEM((NC, KB, D), BF16),
        pltpu.VMEM((NC, R, D), BF16),
        pltpu.VMEM((NC, R, D), BF16),
        pltpu.VMEM((NZ, NY, ZR, D), BF16),
        pltpu.VMEM((NY, R, D), BF16),
        pltpu.VMEM((NY, D, R), BF16),
        pltpu.VMEM((NB, NC, R, KB), BF16),
        pltpu.VMEM((NB, NC, R, KB), BF16),
        pltpu.VMEM((NB, NC, R, KB), BF16),
        pltpu.VMEM((NC, NY, NZ, ZR, KB), BF16),
        pltpu.VMEM((NY, NC, R, KB), BF16),
        pltpu.VMEM((2, NC, R, D), F32),
        pltpu.VMEM((D, KB), F32),
        pltpu.VMEM((D, NY * R), BF16),
        pltpu.VMEM((NB, KB), F32),
        pltpu.VMEM((ITERS, NY, NB, KB), F32),
        pltpu.VMEM((ITERS, NP, 8, 128), F32),
        pltpu.VMEM((ITERS - 1, NC, 8, 128), F32),
        pltpu.VMEM((2, 8, 128), F32),
        pltpu.VMEM((2, 4, 128), F32),
        pltpu.VMEM((NP, 4, 128), F32),
        pltpu.VMEM((NY, 4, 128), F32),
        pltpu.VMEM((NY, 4, 128), F32),
        pltpu.VMEM((2, R, D), BF16),
        pltpu.VMEM((2, R, D), BF16),
        pltpu.VMEM((2, NZ, ZR, D), BF16),
        pltpu.VMEM((2, NZ, ZR, D), BF16),
        pltpu.VMEM((2, NX, 16, D), BF16),
        pltpu.VMEM((2, NX, 16, D), BF16),
        pltpu.VMEM((D, KB), BF16),
        pltpu.VMEM((D, KB), BF16),
        pltpu.VMEM((D, KB), BF16),
        pltpu.VMEM((D, KB), BF16),
        dma((NB + 1,)),
        dma((2,)), dma((2,)),
        dma((ITERS,)), dma((ITERS,)),
        dma((ITERS + 1,)), dma((ITERS + 1,)),
        dma((ITERS + 1,)), dma((ITERS + 1,)),
        dma((1,)), dma((1,)),
        dma((2, 4)), dma((2, 4)),
        dma((2, 4)), dma((2, 4)),
        dma((2,)), dma((2,)),
        dma((2, 3)), dma((2, 3)),
        dma((2,)), dma((2,)),
    ]
    loss, grad_student, grad_proto = pl.pallas_call(
        kernel,
        out_shape=(
            jax.ShapeDtypeStruct((1, R), F32),
            jax.ShapeDtypeStruct((PR, D), F32),
            jax.ShapeDtypeStruct((KB, D), BF16),
        ),
        in_specs=[vmem, vmem, pl.BlockSpec(memory_space=pl.ANY), vmem],
        out_specs=(vmem, vmem, vmem),
        scratch_shapes=scratch,
        compiler_params=pltpu.CompilerParams(
            collective_id=0, has_side_effects=True, vmem_limit_bytes=56 * 2**20
        ),
        name="sinkhorn_head",
    )(teacher_feat, student_feat, prototypes, row_weight.reshape(1, R))
    return (loss.reshape(R), grad_student, grad_proto)


def solution(mesh):
    return jax.shard_map(
        shards,
        mesh=mesh,
        in_specs=(P("dp", None), P("dp", None), P("proto", None), P("dp")),
        out_specs=(P("dp"), P(("dp", "proto"), None), P(("proto", "dp"), None)),
        check_vma=False,
    )
```

```python
import math

import jax
import jax.numpy as jnp
from jax import lax
from jax.experimental import pallas as pl
from jax.experimental.pallas import tpu as pltpu
from jax.sharding import PartitionSpec as P

MESH = pl.DeviceIdType.MESH
F32, BF16 = jnp.float32, jnp.bfloat16
ITERS = 3
NY, NC, NZ, NX = 8, 2, 8, 4
NP = NZ * NX
R = 384
D = 384
KB = 256
NB = 8
ZR = R // NZ
PR = R // NP
EPS = 1e-6
EXPO_SCALE = 25.0 * math.log2(math.e)
NT = (((1,), (1,)), ((), ()))


def hops(step, size):
    return min(step, size - step)


Y_STEPS = sorted(range(1, NY), key=lambda a: -hops(a, NY))
Z_STEPS = sorted(range(1, NZ), key=lambda a: -hops(a, NZ))
X_STEPS = sorted(range(1, NX), key=lambda a: -hops(a, NX))
ZX_STEPS = sorted(
    [(a, b) for a in range(NZ) for b in range(NX) if (a, b) != (0, 0)],
    key=lambda s: -(hops(s[0], NZ) + hops(s[1], NX)),
)


def unit_rows(values):
    floats = values.astype(F32)
    return floats * lax.rsqrt(jnp.sum(floats * floats, axis=-1, keepdims=True) + EPS)


def two_rows(vector):
    high = vector.astype(BF16).astype(F32)
    low = vector - high
    rows = lax.broadcasted_iota(jnp.int32, (16, vector.shape[1]), 0)
    return jnp.where(rows == 0, high, jnp.where(rows == 1, low, 0.0)).astype(BF16)


def pack(vectors, rows):
    parts = [v[:, j : j + 128] for v in vectors for j in range(0, v.shape[1], 128)]
    if len(parts) < rows:
        parts.append(jnp.zeros((rows - len(parts), 128), F32))
    return jnp.concatenate(parts, axis=0)


def unpack(tile, start, count):
    return jnp.concatenate([tile[j : j + 1, :] for j in range(start, start + count)], axis=1)


def kernel(
    t_ref, s_ref, w_ref, rw_ref, loss_ref, gs_ref, gp_ref,
    wraw, wfraw, wn, wnt, wnf, tn2, sn2, gt, gs, snt, expo, expoz, prob, ef, pf, uw,
    vacc, scaled, cvec, ybuf, zxbuf, cbuf, c3buf, auxc, auxzx, abuf, bbuf,
    ucs, ucr, uzs, uzr, uxs, uxr, vsend, vrecv, bsend, brecv,
    wsem, xs, xr, ys, yr, zxs, zxr, cs, cr, gts, gtr, tcs, tcr, scs, scr, abs_, abr,
    us, ur, vbs, vbr,
):
    dp, pr = lax.axis_index("dp"), lax.axis_index("proto")
    y, c = lax.div(dp, NC), lax.rem(dp, NC)
    z, x = lax.div(pr, NX), lax.rem(pr, NX)
    o = 1 - c

    def dev(yy, cc, zz, xx):
        return {"dp": yy * NC + cc, "proto": zz * NX + xx}

    sibling = dev(y, o, z, x)
    y_at = lambda a: lax.rem(y + a, NY)
    z_at = lambda a: lax.rem(z + a, NZ)
    x_at = lambda a: lax.rem(x + a, NX)
    late = []

    def wait_for(ref, sem):
        pltpu.make_async_copy(ref, ref, sem).wait()

    def send(src, dst, ss, rs, to):
        pltpu.make_async_remote_copy(
            src_ref=src, dst_ref=dst, send_sem=ss, recv_sem=rs, device_id=to, device_id_type=MESH
        ).start()

    def send_y(ref, ss, rs):
        for a in Y_STEPS:
            send(ref.at[y], ref.at[y], ss, rs, dev(y_at(a), c, z, x))
        late.append((ref.at[pl.ds(0, NY - 1)], ss))

    def send_zx(ref, ss, rs):
        for a, b in ZX_STEPS:
            send(ref.at[pr], ref.at[pr], ss, rs, dev(y, c, z_at(a), x_at(b)))
        late.append((ref.at[pl.ds(0, NP - 1)], ss))

    def send_core(src, dst, ss, rs):
        send(src, dst, ss, rs, sibling)
        late.append((src, ss))

    loads = [
        pltpu.make_async_copy(w_ref.at[pl.ds((2 * b + c) * KB, KB)], wraw.at[b], wsem.at[b])
        for b in range(NB)
    ]
    loads.append(pltpu.make_async_copy(w_ref.at[pl.ds(2 * y * KB, 2 * KB)], wfraw, wsem.at[NB]))
    for load in loads:
        load.start()
    barrier = pltpu.get_barrier_semaphore()
    peers = [sibling]
    peers += [dev(y, c, z_at(a), x_at(b)) for a, b in ZX_STEPS]
    peers += [dev(y_at(a), c, z, x) for a in Y_STEPS]
    for peer in peers:
        pl.semaphore_signal(barrier, inc=1, device_id=peer, device_id_type=MESH)

    tn_own = unit_rows(t_ref[...]).astype(BF16)
    tn2[c] = tn_own

    def expo_block(b, h):
        e = jnp.exp2(lax.dot_general(tn2[h], wn[b], NT, preferred_element_type=F32) * EXPO_SCALE)
        expo[b, h] = e.astype(BF16)
        return jnp.sum(e, axis=0, keepdims=True)

    for b in range(NB):
        loads[b].wait()
        wn[b] = unit_rows(wraw[b]).astype(BF16)
        ybuf[0, y, b : b + 1, :] = expo_block(b, c)
    sn_own = unit_rows(s_ref[...]).astype(BF16)
    sn2[c] = sn_own

    pl.semaphore_wait(barrier, len(peers))
    send_core(tn2.at[c], tn2.at[c], xs.at[0], xr.at[0])
    gt[z, y] = tn2[c, pl.ds(pl.multiple_of(z * ZR, 16), ZR), :]
    for a in Y_STEPS:
        send(gt.at[z, y], gt.at[z, y], gts.at[0], gtr.at[0], dev(y_at(a), c, z, x))
    late.append((gt.at[0, pl.ds(0, NY - 1)], gts.at[0]))
    send_core(sn2.at[c], sn2.at[c], xs.at[1], xr.at[1])
    gs[y] = sn_own

    def student_block(b, h):
        zs = lax.dot_general(sn2[h], wn[b], NT, preferred_element_type=F32) * 10.0
        prob[b, h] = jnp.exp(zs).astype(BF16)
        expoz[b, h] = (expo[b, h].astype(F32) * zs).astype(BF16)

    for b in range(NB // 2):
        student_block(b, c)
    wait_for(tn2.at[o], xr.at[0])
    for b in range(NB):
        ybuf[0, y, b : b + 1, :] += expo_block(b, o)

    def y_chain(step):
        if step > 1:
            for way, back in ((0, -(step - 1)), (1, step - 1)):
                wait_for(gs.at[y_at(NY + back)], scr.at[way, step - 2])
        for way, back, to in ((0, -(step - 1), 1), (1, step - 1, -1)):
            src = gs.at[y_at(NY + back)]
            if step == 4:
                src = src.at[pl.ds(way * (R // 2), R // 2)]
            send(src, src, scs.at[way, step - 1], scr.at[way, step - 1], dev(y_at(NY + to), c, z, x))
            late.append((src, scs.at[way, step - 1]))

    def y_chain_end():
        for way in range(2):
            wait_for(gs.at[y_at(4), pl.ds(way * (R // 2), R // 2)], scr.at[way, 3])

    def z_chain(step):
        if step == 1:
            wait_for(gt.at[z, pl.ds(0, NY - 1)], gtr.at[0])
        else:
            for way, back in ((0, -(step - 1)), (1, step - 1)):
                wait_for(gt.at[z_at(NZ + back)], tcr.at[way, step - 2])
        for way, back, to in ((0, -(step - 1), 1), (1, step - 1, -1)):
            src = gt.at[z_at(NZ + back)]
            if step == 4:
                src = src.at[pl.ds(way * (NY // 2), NY // 2)]
            send(src, src, tcs.at[way, step - 1], tcr.at[way, step - 1], dev(y, c, z_at(NZ + to), x))
            late.append((src, tcs.at[way, step - 1]))

    def z_chain_end():
        for way in range(2):
            wait_for(gt.at[z_at(4), pl.ds(way * (NY // 2), NY // 2)], tcr.at[way, 3])

    def fill_teacher(slice_):
        rows = gt[slice_].reshape(R, D)
        for h in range(NC):
            st = lax.dot_general(rows, wnf[h], NT, preferred_element_type=F32)
            e = jnp.exp2(st * EXPO_SCALE).astype(BF16)
            for g in range(NY):
                ef[h, g, slice_] = e[g * ZR : (g + 1) * ZR]

    def fill_student(group):
        rows = gs[group]
        snt[group] = rows.T
        for h in range(NC):
            zs = lax.dot_general(rows, wnf[h], NT, preferred_element_type=F32) * 10.0
            pf[group, h] = jnp.exp(zs).astype(BF16)

    def own(v):
        return jnp.where(c == 0, v[:, :R], v[:, R:])

    def other(v):
        return jnp.where(c == 0, v[:, R:], v[:, :R])

    def row_sums(lhs, mats):
        sums = [jnp.zeros((16, NC * R), F32) for _ in mats]
        for b in range(NB):
            left = lhs(b)
            for i, mat in enumerate(mats):
                sums[i] = sums[i] + lax.dot_general(
                    left, mat[b].reshape(NC * R, KB), NT, preferred_element_type=F32
                )
        return [s[0:1] + s[1:2] for s in sums]

    def sum_protos(q, mat, scale):
        def half(h, carry):
            left = jnp.concatenate([mat[b, h] for b in range(NB)], axis=1)
            if scale is None:
                right = jnp.concatenate([wnt[b] for b in range(NB)], axis=1)
            else:
                right = jnp.concatenate(
                    [(wnt[b].astype(F32) * scale[b : b + 1, :]).astype(BF16) for b in range(NB)], axis=1
                )
            uw[q, h] = lax.dot_general(left, right, NT, preferred_element_type=F32)
            return carry

        lax.fori_loop(0, NC, half, 0)
        ucs[q] = uw[q, o].astype(BF16)
        send_core(ucs.at[q], ucr.at[q], us.at[q, 0], ur.at[q, 0])

    def student_x(q):
        wait_for(ucr.at[q], ur.at[q, 0])
        total = uw[q, c] + ucr[q].astype(F32)
        pad = jnp.zeros((16 - PR, D), F32)
        for i in range(NP):
            tile = jnp.concatenate([total[i * PR : (i + 1) * PR], pad], axis=0)
            uxs[q, i % NX, i // NX] = tile.astype(BF16)
        uxr[q, x] = uxs[q, x]
        for a in X_STEPS:
            send(uxs.at[q, x_at(a)], uxr.at[q, x], us.at[q, 1], ur.at[q, 1], dev(y, c, z, x_at(a)))
        late.append((uxs.at[q, pl.ds(0, NX - 1)], us.at[q, 1]))

    def student_z(q):
        wait_for(uxr.at[q, pl.ds(0, NX - 1)], ur.at[q, 1])
        uzs[q] = jnp.sum(uxr[q].astype(F32), axis=0).astype(BF16)
        uzr[q, z] = uzs[q, z]
        for a in Z_STEPS:
            send(uzs.at[q, z_at(a)], uzr.at[q, z], us.at[q, 2], ur.at[q, 2], dev(y, c, z_at(a), x))
        late.append((uzs.at[q, pl.ds(0, NZ - 1)], us.at[q, 2]))

    def student_end(q):
        wait_for(uzr.at[q, pl.ds(0, NZ - 1)], ur.at[q, 2])
        return jnp.sum(uzr[q].astype(F32), axis=0)

    rowscale = None
    for it in range(ITERS):
        last = it == ITERS - 1
        if it > 0:
            left = two_rows(rowscale)
            for b in range(NB):
                both = jnp.dot(left, expo[b].reshape(NC * R, KB), preferred_element_type=F32)
                ybuf[it, y, b : b + 1, :] = both[0:1] + both[1:2]
        send_y(ybuf.at[it], ys.at[it], yr.at[it])
        if it == 0:
            y_chain(1)
            for b in range(NB // 2, NB):
                student_block(b, c)
            wait_for(sn2.at[o], xr.at[1])
            for b in range(NB):
                student_block(b, o)
            z_chain(1)
        elif it == 1:
            wait_for(auxc.at[1], cr.at[ITERS])
            auxzx[pr] = pack([expsum_own], 4) + auxc[1]
            send_zx(auxzx, zxs.at[ITERS], zxr.at[ITERS])
            y_chain(2)
            z_chain(2)
            fill_student(y_at(1))
            fill_student(y_at(NY - 1))
        else:
            wait_for(auxzx.at[pl.ds(0, NP - 1)], zxr.at[ITERS])
            expsum = unpack(jnp.sum(auxzx[...], axis=0), 0, 3)
            lse = jnp.log(expsum)
            weight = rw_ref[...].reshape(1, R) * 10.0
            alpha = weight / expsum
            abuf[y] = pack([alpha], 4)
            send_y(abuf, abs_.at[0], abr.at[0])
            student_z(0)
            fill_student(y_at(2))
            fill_student(y_at(NY - 2))
            fill_teacher(z_at(2))
            fill_teacher(z_at(NZ - 2))
            y_chain(4)
            z_chain(4)
        wait_for(ybuf.at[it, pl.ds(0, NY - 1)], yr.at[it])
        colscale = 1.0 / jnp.sum(ybuf[it], axis=0)
        cvec[...] = colscale
        if not last:
            (tot,) = row_sums(lambda b: two_rows(cvec[b : b + 1, :]), [expo])
            zxbuf[it, pr] = pack([tot], 8)
        else:
            tot, qz = row_sums(lambda b: two_rows(cvec[b : b + 1, :]), [expo, expoz])
            c3buf[0] = pack([other(tot), other(qz)], 8)
            send_core(c3buf.at[0], c3buf.at[1], cs.at[it], cr.at[it])
            mine = pack([own(tot), own(qz)], 8)
            wait_for(c3buf.at[1], cr.at[it])
            zxbuf[it, pr] = mine + c3buf[1]
        send_zx(zxbuf.at[it], zxs.at[it], zxr.at[it])
        if it == 0:
            rows16 = lax.broadcasted_iota(jnp.int32, (16, KB), 0)
            ones = jnp.where(rows16 == 0, 1.0, 0.0).astype(BF16)
            (expsum,) = row_sums(lambda b: ones, [prob])
            auxc[0] = pack([other(expsum)], 4)
            send_core(auxc.at[0], auxc.at[1], cs.at[ITERS], cr.at[ITERS])
            expsum_own = own(expsum)
            for b in range(NB):
                wnt[b] = wn[b].T
            sum_protos(0, prob, None)
            loads[NB].wait()
            for h in range(NC):
                wnf[h] = unit_rows(wfraw[pl.ds(h * KB, KB), :]).astype(BF16)
            fill_student(y)
        elif it == 1:
            fill_teacher(z)
            fill_teacher(z_at(1))
            fill_teacher(z_at(NZ - 1))
            student_x(0)
            y_chain(3)
            z_chain(3)
        else:
            sum_protos(1, expo, colscale)
            fill_student(y_at(3))
            fill_student(y_at(NY - 3))
            fill_teacher(z_at(3))
            fill_teacher(z_at(NZ - 3))
            student_x(1)
        wait_for(zxbuf.at[it, pl.ds(0, NP - 1)], zxr.at[it])
        sums = jnp.sum(zxbuf[it], axis=0)
        if not last:
            cbuf[it, c] = sums
            send_core(cbuf.at[it, c], cbuf.at[it, c], cs.at[it], cr.at[it])
            wait_for(cbuf.at[it, o], cr.at[it])
            rowscale = 1.0 / unpack(cbuf[it, 0] + cbuf[it, 1], 0, 6)
    rowscale = 1.0 / unpack(sums, 0, 3)
    loss_ref[...] = (lse - rowscale * unpack(sums, 3, 3)).reshape(R)
    beta = weight * rowscale
    bbuf[y] = pack([beta], 4)
    send_y(bbuf, abs_.at[1], abr.at[1])

    y_chain_end()
    z_chain_end()
    fill_student(y_at(4))
    fill_teacher(z_at(4))
    wait_for(abuf.at[pl.ds(0, NY - 1)], abr.at[0])

    def scale_students(buf):
        for g in range(NY):
            factor = unpack(buf[g], 0, 3)
            scaled[:, g * R : (g + 1) * R] = (snt[g].astype(F32) * factor).astype(BF16)

    scale_students(abuf)

    def student_part(h):
        right = jnp.concatenate([pf[g, h] for g in range(NY)], axis=0)
        return jnp.dot(scaled[...], right, preferred_element_type=F32)

    def teacher_part(h):
        right = ef[h].reshape(NY * R, KB)
        return jnp.dot(scaled[...], right, preferred_element_type=F32)

    vsend[...] = student_part(o).astype(BF16)
    send_core(vsend, vrecv, vbs.at[0], vbr.at[0])
    vacc[...] = student_part(c)
    wait_for(bbuf.at[pl.ds(0, NY - 1)], abr.at[1])
    scale_students(bbuf)
    bsend[...] = teacher_part(o).astype(BF16)
    send_core(bsend, brecv, vbs.at[1], vbr.at[1])
    student_z(1)
    teacher = teacher_part(c)

    wait_for(vrecv, vbr.at[0])
    wait_for(brecv, vbr.at[1])
    xg = vacc[...] + vrecv[...].astype(F32) - cvec[pl.ds(y, 1), :] * (teacher + brecv[...].astype(F32))
    xg = xg.T
    floats = wraw[y].astype(F32)
    inv = lax.rsqrt(jnp.sum(floats * floats, axis=1, keepdims=True) + EPS)
    unit = floats * inv
    gp_ref[...] = ((xg - unit * jnp.sum(unit * xg, axis=1, keepdims=True)) * inv).astype(BF16)

    rows = lax.broadcasted_iota(jnp.int32, (16, R), 0)
    lanes = lax.broadcasted_iota(jnp.int32, (16, R), 1)
    pick = jnp.where((lanes == rows + pr * PR) & (rows < PR), 1.0, 0.0)
    dsn = jnp.sum(pick * alpha, axis=1, keepdims=True) * student_end(0)
    dsn = dsn - jnp.sum(pick * beta, axis=1, keepdims=True) * student_end(1)
    mine = jnp.dot(pick.astype(BF16), s_ref[...], preferred_element_type=F32)
    inv = lax.rsqrt(jnp.sum(mine * mine, axis=1, keepdims=True) + EPS)
    mine = mine * inv
    grad = (dsn - mine * jnp.sum(mine * dsn, axis=1, keepdims=True)) * inv
    gs_ref[...] = grad[:PR]

    for ref, sem in late:
        wait_for(ref, sem)


def write_outputs(loss_in, gs_in, gp_in, loss_ref, gs_ref, gp_ref):
    loss_ref[...] = loss_in[...]
    gs_ref[...] = gs_in[...]
    gp_ref[...] = gp_in[...]


def shards(teacher_feat, student_feat, prototypes, row_weight):
    vmem = pl.BlockSpec(memory_space=pltpu.VMEM)
    anywhere = pl.BlockSpec(memory_space=pl.ANY)
    dma = pltpu.SemaphoreType.DMA
    scratch = [
        pltpu.VMEM((NB, KB, D), BF16),
        pltpu.VMEM((2 * KB, D), BF16),
        pltpu.VMEM((NB, KB, D), BF16),
        pltpu.VMEM((NB, D, KB), BF16),
        pltpu.VMEM((NC, KB, D), BF16),
        pltpu.VMEM((NC, R, D), BF16),
        pltpu.VMEM((NC, R, D), BF16),
        pltpu.VMEM((NZ, NY, ZR, D), BF16),
        pltpu.VMEM((NY, R, D), BF16),
        pltpu.VMEM((NY, D, R), BF16),
        pltpu.VMEM((NB, NC, R, KB), BF16),
        pltpu.VMEM((NB, NC, R, KB), BF16),
        pltpu.VMEM((NB, NC, R, KB), BF16),
        pltpu.VMEM((NC, NY, NZ, ZR, KB), BF16),
        pltpu.VMEM((NY, NC, R, KB), BF16),
        pltpu.VMEM((2, NC, R, D), F32),
        pltpu.VMEM((D, KB), F32),
        pltpu.VMEM((D, NY * R), BF16),
        pltpu.VMEM((NB, KB), F32),
        pltpu.VMEM((ITERS, NY, NB, KB), F32),
        pltpu.VMEM((ITERS, NP, 8, 128), F32),
        pltpu.VMEM((ITERS - 1, NC, 8, 128), F32),
        pltpu.VMEM((2, 8, 128), F32),
        pltpu.VMEM((2, 4, 128), F32),
        pltpu.VMEM((NP, 4, 128), F32),
        pltpu.VMEM((NY, 4, 128), F32),
        pltpu.VMEM((NY, 4, 128), F32),
        pltpu.VMEM((2, R, D), BF16),
        pltpu.VMEM((2, R, D), BF16),
        pltpu.VMEM((2, NZ, 16, D), BF16),
        pltpu.VMEM((2, NZ, 16, D), BF16),
        pltpu.VMEM((2, NX, NZ, 16, D), BF16),
        pltpu.VMEM((2, NX, NZ, 16, D), BF16),
        pltpu.VMEM((D, KB), BF16),
        pltpu.VMEM((D, KB), BF16),
        pltpu.VMEM((D, KB), BF16),
        pltpu.VMEM((D, KB), BF16),
        dma((NB + 1,)),
        dma((2,)), dma((2,)),
        dma((ITERS,)), dma((ITERS,)),
        dma((ITERS + 1,)), dma((ITERS + 1,)),
        dma((ITERS + 1,)), dma((ITERS + 1,)),
        dma((1,)), dma((1,)),
        dma((2, 4)), dma((2, 4)),
        dma((2, 4)), dma((2, 4)),
        dma((2,)), dma((2,)),
        dma((2, 3)), dma((2, 3)),
        dma((2,)), dma((2,)),
    ]
    loss, grad_student, grad_proto = pl.pallas_call(
        kernel,
        out_shape=(
            jax.ShapeDtypeStruct((R,), F32),
            jax.ShapeDtypeStruct((PR, D), F32),
            jax.ShapeDtypeStruct((KB, D), BF16),
        ),
        in_specs=[vmem, vmem, anywhere, vmem],
        out_specs=(vmem, vmem, vmem),
        scratch_shapes=scratch,
        compiler_params=pltpu.CompilerParams(
            collective_id=0, has_side_effects=True, vmem_limit_bytes=56 * 2**20
        ),
        name="sinkhorn_head",
    )(teacher_feat, student_feat, prototypes, row_weight)
    return pl.pallas_call(
        write_outputs,
        out_shape=(
            jax.ShapeDtypeStruct((R,), F32),
            jax.ShapeDtypeStruct((PR, D), F32),
            jax.ShapeDtypeStruct((KB, D), BF16),
        ),
        in_specs=[vmem] * 3,
        out_specs=(vmem,) * 3,
        name="write_outputs",
    )(loss, grad_student, grad_proto)


def solution(mesh):
    return jax.shard_map(
        shards,
        mesh=mesh,
        in_specs=(P("dp", None), P("dp", None), P("proto", None), P("dp")),
        out_specs=(P("dp"), P(("dp", "proto"), None), P(("proto", "dp"), None)),
        check_vma=False,
    )
```

```python
import math

import jax
import jax.numpy as jnp
from jax import lax
from jax.experimental import pallas as pl
from jax.experimental.pallas import tpu as pltpu
from jax.sharding import PartitionSpec as P

MESH = pl.DeviceIdType.MESH
F32, BF16 = jnp.float32, jnp.bfloat16
ITERS = 3
NY, NC, NZ, NX = 8, 2, 8, 4
NP = NZ * NX
R = 384
D = 384
KB = 256
NB = 8
PIECE = 32
PIECES = R // PIECE
PR = R // NP
EPS = 1e-6
EXPO_SCALE = 25.0 * math.log2(math.e)
NT = (((1,), (1,)), ((), ()))


def hops(step, size):
    return min(step, size - step)


Y_STEPS = sorted(range(1, NY), key=lambda a: -hops(a, NY))
Z_STEPS = sorted(range(1, NZ), key=lambda a: -hops(a, NZ))
X_STEPS = sorted(range(1, NX), key=lambda a: -hops(a, NX))
ZX_STEPS = sorted(
    [(a, b) for a in range(NZ) for b in range(NX) if (a, b) != (0, 0)],
    key=lambda s: -(hops(s[0], NZ) + hops(s[1], NX)),
)


def unit_rows(values):
    floats = values.astype(F32)
    return floats * lax.rsqrt(jnp.sum(floats * floats, axis=-1, keepdims=True) + EPS)


def two_rows(vector):
    high = vector.astype(BF16).astype(F32)
    low = vector - high
    rows = lax.broadcasted_iota(jnp.int32, (16, vector.shape[1]), 0)
    return jnp.where(rows == 0, high, jnp.where(rows == 1, low, 0.0)).astype(BF16)


def pack(vectors, rows):
    parts = [v[:, j : j + 128] for v in vectors for j in range(0, v.shape[1], 128)]
    if len(parts) < rows:
        parts.append(jnp.zeros((rows - len(parts), 128), F32))
    return jnp.concatenate(parts, axis=0)


def unpack(tile, start, count):
    return jnp.concatenate([tile[j : j + 1, :] for j in range(start, start + count)], axis=1)


def kernel(
    t_ref, s_ref, w_ref, rw_ref, loss_ref, gs_ref, gp_ref,
    wraw, wfraw, wn, wnt, wnf, tn2, sn2, gt, gs, snt, expo, expoz, prob, ef, pf, uw,
    vacc, scaled, cvec, ybuf, zxbuf, cbuf, c3buf, auxc, auxzx, abuf, bbuf,
    ucs, ucr, uzs, uzr, uxs, uxr, vsend, vrecv, bsend, brecv,
    wsem, xs, xr, ys, yr, zxs, zxr, cs, cr, gts, gtr, tcs, tcr, hcs, hcr, scs, scr, abs_, abr,
    us, ur, vbs, vbr,
):
    dp, pr = lax.axis_index("dp"), lax.axis_index("proto")
    y, c = lax.div(dp, NC), lax.rem(dp, NC)
    z, x = lax.div(pr, NX), lax.rem(pr, NX)
    o = 1 - c

    def dev(yy, cc, zz, xx):
        return {"dp": yy * NC + cc, "proto": zz * NX + xx}

    sibling = dev(y, o, z, x)
    y_at = lambda a: lax.rem(y + a, NY)
    z_at = lambda a: lax.rem(z + a, NZ)
    x_at = lambda a: lax.rem(x + a, NX)
    late = []

    def wait_for(ref, sem):
        pltpu.make_async_copy(ref, ref, sem).wait()

    def send(src, dst, ss, rs, to):
        pltpu.make_async_remote_copy(
            src_ref=src, dst_ref=dst, send_sem=ss, recv_sem=rs, device_id=to, device_id_type=MESH
        ).start()

    def send_y(ref, ss, rs):
        for a in Y_STEPS:
            send(ref.at[y], ref.at[y], ss, rs, dev(y_at(a), c, z, x))
        late.append((ref.at[pl.ds(0, NY - 1)], ss))

    def send_zx(ref, ss, rs):
        for a, b in ZX_STEPS:
            send(ref.at[pr], ref.at[pr], ss, rs, dev(y, c, z_at(a), x_at(b)))
        late.append((ref.at[pl.ds(0, NP - 1)], ss))

    def send_core(src, dst, ss, rs):
        send(src, dst, ss, rs, sibling)
        late.append((src, ss))

    loads = [
        pltpu.make_async_copy(w_ref.at[pl.ds((2 * b + c) * KB, KB)], wraw.at[b], wsem.at[b])
        for b in range(NB)
    ]
    loads.append(pltpu.make_async_copy(w_ref.at[pl.ds(2 * y * KB, 2 * KB)], wfraw, wsem.at[NB]))
    for load in loads:
        load.start()
    barrier = pltpu.get_barrier_semaphore()
    peers = [sibling]
    peers += [dev(y, c, z_at(a), x_at(b)) for a, b in ZX_STEPS]
    peers += [dev(y_at(a), c, z, x) for a in Y_STEPS]
    for peer in peers:
        pl.semaphore_signal(barrier, inc=1, device_id=peer, device_id_type=MESH)

    tn_own = unit_rows(t_ref[...]).astype(BF16)
    tn2[c] = tn_own

    def expo_block(b, h):
        e = jnp.exp2(lax.dot_general(tn2[h], wn[b], NT, preferred_element_type=F32) * EXPO_SCALE)
        expo[b, h] = e.astype(BF16)
        return jnp.sum(e, axis=0, keepdims=True)

    for b in range(NB):
        loads[b].wait()
        wn[b] = unit_rows(wraw[b]).astype(BF16)
        ybuf[0, y, b : b + 1, :] = expo_block(b, c)
    sn_own = unit_rows(s_ref[...]).astype(BF16)
    sn2[c] = sn_own
    for b in range(NB):
        wnt[b] = wn[b].T
    loads[NB].wait()
    for h in range(NC):
        wnf[h] = unit_rows(wfraw[pl.ds(h * KB, KB), :]).astype(BF16)

    def y_chain(step):
        if step > 1:
            for way, back in ((0, -(step - 1)), (1, step - 1)):
                wait_for(gs.at[y_at(NY + back)], scr.at[way, step - 2])
        for way, back, to in ((0, -(step - 1), 1), (1, step - 1, -1)):
            src = gs.at[y_at(NY + back)]
            if step == 4:
                src = src.at[pl.ds(way * (R // 2), R // 2)]
            send(src, src, scs.at[way, step - 1], scr.at[way, step - 1], dev(y_at(NY + to), c, z, x))
            late.append((src, scs.at[way, step - 1]))

    def y_chain_end():
        for way in range(2):
            wait_for(gs.at[y_at(4), pl.ds(way * (R // 2), R // 2)], scr.at[way, 3])

    def z_chain(step):
        if step == 1:
            wait_for(gt.at[z, pl.ds(0, NY - 1)], gtr.at[0])
        else:
            for way, back in ((0, -(step - 1)), (1, step - 1)):
                wait_for(gt.at[z_at(NZ + back)], tcr.at[way, step - 2])
        for way, back, to in ((0, -(step - 1), 1), (1, step - 1, -1)):
            src = gt.at[z_at(NZ + back)]
            if step == 4:
                src = src.at[pl.ds(way * (NY // 2), NY // 2)]
            send(src, src, tcs.at[way, step - 1], tcr.at[way, step - 1], dev(y, c, z_at(NZ + to), x))
            late.append((src, tcs.at[way, step - 1]))

    def z_chain_end():
        for way in range(2):
            wait_for(gt.at[z_at(4), pl.ds(way * (NY // 2), NY // 2)], tcr.at[way, 3])

    def x_chain(step):
        if step == 1:
            wait_for(gt.at[NZ + x, pl.ds(0, NY - 1)], gtr.at[1])
        else:
            for way, back in ((0, -1), (1, 1)):
                wait_for(gt.at[NZ + x_at(NX + back)], hcr.at[way, 0])
        for way, back, to in ((0, -(step - 1), 1), (1, step - 1, -1)):
            src = gt.at[NZ + x_at(NX + back)]
            if step == 2:
                src = src.at[pl.ds(way * (NY // 2), NY // 2)]
            send(src, src, hcs.at[way, step - 1], hcr.at[way, step - 1], dev(y, c, z, x_at(NX + to)))
            late.append((src, hcs.at[way, step - 1]))

    def x_chain_end():
        for way in range(2):
            wait_for(gt.at[NZ + x_at(2), pl.ds(way * (NY // 2), NY // 2)], hcr.at[way, 1])

    pl.semaphore_wait(barrier, len(peers))
    send_core(tn2.at[c], tn2.at[c], xs.at[0], xr.at[0])
    gs[y] = sn_own
    send_core(sn2.at[c], sn2.at[c], xs.at[1], xr.at[1])

    def spread_teacher(i):
        piece = (z, NZ + x)[i]
        gt[piece, y] = tn2[c, pl.ds(pl.multiple_of(piece * PIECE, PIECE), PIECE), :]
        for a in Y_STEPS:
            send(gt.at[piece, y], gt.at[piece, y], gts.at[i], gtr.at[i], dev(y_at(a), c, z, x))
        late.append((gt.at[0, pl.ds(0, NY - 1)], gts.at[i]))

    def student_block(b, h):
        zs = lax.dot_general(sn2[h], wn[b], NT, preferred_element_type=F32) * 10.0
        prob[b, h] = jnp.exp(zs).astype(BF16)
        expoz[b, h] = (expo[b, h].astype(F32) * zs).astype(BF16)

    for b in range(NB // 2):
        student_block(b, c)
    wait_for(tn2.at[o], xr.at[0])
    for b in range(NB):
        ybuf[0, y, b : b + 1, :] += expo_block(b, o)

    def fill_teacher(piece):
        rows = gt[piece].reshape(NY * PIECE, D)
        for h in range(NC):
            st = lax.dot_general(rows, wnf[h], NT, preferred_element_type=F32)
            e = jnp.exp2(st * EXPO_SCALE).astype(BF16)
            for g in range(NY):
                ef[h, g, piece] = e[g * PIECE : (g + 1) * PIECE]

    def fill_student(group):
        rows = gs[group]
        snt[group] = rows.T
        for h in range(NC):
            zs = lax.dot_general(rows, wnf[h], NT, preferred_element_type=F32) * 10.0
            pf[group, h] = jnp.exp(zs).astype(BF16)

    def own(v):
        return jnp.where(c == 0, v[:, :R], v[:, R:])

    def other(v):
        return jnp.where(c == 0, v[:, R:], v[:, :R])

    def row_sums(mat, scale, matmuls):
        total = jnp.zeros((16, NC * R), F32)
        lanes = jnp.zeros((NC * R, 128), F32)
        for b in range(NB):
            block = mat[b].reshape(NC * R, KB)
            if b < matmuls:
                total = total + lax.dot_general(
                    two_rows(scale[b : b + 1, :]), block, NT, preferred_element_type=F32
                )
            else:
                block = block.astype(F32)
                if scale is not None:
                    block = block * scale[b : b + 1, :]
                lanes = lanes + (block[:, :128] + block[:, 128:])
        vector = jnp.sum(lanes.T, axis=0, keepdims=True)
        return vector + total[0:1] + total[1:2] if matmuls else vector

    def sum_protos(q, mat, scale):
        def half(h, carry):
            left = jnp.concatenate([mat[b, h] for b in range(NB)], axis=1)
            if scale is None:
                right = jnp.concatenate([wnt[b] for b in range(NB)], axis=1)
            else:
                right = jnp.concatenate(
                    [(wnt[b].astype(F32) * scale[b : b + 1, :]).astype(BF16) for b in range(NB)], axis=1
                )
            uw[q, h] = lax.dot_general(left, right, NT, preferred_element_type=F32)
            return carry

        lax.fori_loop(0, NC, half, 0)
        ucs[q] = uw[q, o].astype(BF16)
        send_core(ucs.at[q], ucr.at[q], us.at[q, 0], ur.at[q, 0])

    def student_x(q):
        wait_for(ucr.at[q], ur.at[q, 0])
        total = uw[q, c] + ucr[q].astype(F32)
        pad = jnp.zeros((16 - PR, D), F32)
        for i in range(NP):
            tile = jnp.concatenate([total[i * PR : (i + 1) * PR], pad], axis=0)
            uxs[q, i % NX, i // NX] = tile.astype(BF16)
        uxr[q, x] = uxs[q, x]
        for a in X_STEPS:
            send(uxs.at[q, x_at(a)], uxr.at[q, x], us.at[q, 1], ur.at[q, 1], dev(y, c, z, x_at(a)))
        late.append((uxs.at[q, pl.ds(0, NX - 1)], us.at[q, 1]))

    def student_z(q):
        wait_for(uxr.at[q, pl.ds(0, NX - 1)], ur.at[q, 1])
        uzs[q] = jnp.sum(uxr[q].astype(F32), axis=0).astype(BF16)
        uzr[q, z] = uzs[q, z]
        for a in Z_STEPS:
            send(uzs.at[q, z_at(a)], uzr.at[q, z], us.at[q, 2], ur.at[q, 2], dev(y, c, z_at(a), x))
        late.append((uzs.at[q, pl.ds(0, NZ - 1)], us.at[q, 2]))

    def student_end(q):
        wait_for(uzr.at[q, pl.ds(0, NZ - 1)], ur.at[q, 2])
        return jnp.sum(uzr[q].astype(F32), axis=0)

    rowscale = None
    for it in range(ITERS):
        last = it == ITERS - 1
        if it > 0:
            left = two_rows(rowscale)
            for b in range(NB):
                both = jnp.dot(left, expo[b].reshape(NC * R, KB), preferred_element_type=F32)
                ybuf[it, y, b : b + 1, :] = both[0:1] + both[1:2]
        send_y(ybuf.at[it], ys.at[it], yr.at[it])
        if it == 0:
            for b in range(NB // 2, NB):
                student_block(b, c)
            wait_for(sn2.at[o], xr.at[1])
            for b in range(NB):
                student_block(b, o)
        elif it == 1:
            wait_for(auxc.at[1], cr.at[ITERS])
            auxzx[pr] = pack([expsum_own], 4) + auxc[1]
            send_zx(auxzx, zxs.at[ITERS], zxr.at[ITERS])
            fill_teacher(z)
            y_chain(2)
            fill_student(y_at(1))
            fill_student(y_at(NY - 1))
        else:
            wait_for(auxzx.at[pl.ds(0, NP - 1)], zxr.at[ITERS])
            expsum = unpack(jnp.sum(auxzx[...], axis=0), 0, 3)
            lse = jnp.log(expsum)
            weight = rw_ref[...].reshape(1, R) * 10.0
            alpha = weight / expsum
            abuf[y] = pack([alpha], 4)
            send_y(abuf, abs_.at[0], abr.at[0])
            student_z(0)
            fill_teacher(z_at(2))
            fill_teacher(z_at(NZ - 2))
            fill_teacher(NZ + x)
        wait_for(ybuf.at[it, pl.ds(0, NY - 1)], yr.at[it])
        if it == 0:
            spread_teacher(0)
            y_chain(1)
        elif it == 1:
            z_chain(2)
            spread_teacher(1)
        else:
            y_chain(4)
            z_chain(4)
            x_chain(2)
        colscale = 1.0 / jnp.sum(ybuf[it], axis=0)
        cvec[...] = colscale
        if not last:
            tot = row_sums(expo, colscale, 3)
            zxbuf[it, pr] = pack([tot], 8)
        else:
            tot = row_sums(expo, colscale, 3)
            qz = row_sums(expoz, colscale, 3)
            c3buf[0] = pack([other(tot), other(qz)], 8)
            send_core(c3buf.at[0], c3buf.at[1], cs.at[it], cr.at[it])
            mine = pack([own(tot), own(qz)], 8)
            wait_for(c3buf.at[1], cr.at[it])
            zxbuf[it, pr] = mine + c3buf[1]
        send_zx(zxbuf.at[it], zxs.at[it], zxr.at[it])
        if it == 0:
            expsum = row_sums(prob, None, 0)
            auxc[0] = pack([other(expsum)], 4)
            send_core(auxc.at[0], auxc.at[1], cs.at[ITERS], cr.at[ITERS])
            expsum_own = own(expsum)
            sum_protos(0, prob, None)
            fill_student(y)
        elif it == 1:
            student_x(0)
            fill_teacher(z_at(1))
            fill_teacher(z_at(NZ - 1))
            y_chain(3)
            fill_student(y_at(2))
            fill_student(y_at(NY - 2))
        else:
            sum_protos(1, expo, colscale)
            fill_student(y_at(3))
            fill_student(y_at(NY - 3))
            student_x(1)
            fill_teacher(z_at(3))
            fill_teacher(z_at(NZ - 3))
        wait_for(zxbuf.at[it, pl.ds(0, NP - 1)], zxr.at[it])
        sums = jnp.sum(zxbuf[it], axis=0)
        if not last:
            cbuf[it, c] = sums
            send_core(cbuf.at[it, c], cbuf.at[it, c], cs.at[it], cr.at[it])
            if it == 0:
                z_chain(1)
            else:
                z_chain(3)
                x_chain(1)
            wait_for(cbuf.at[it, o], cr.at[it])
            rowscale = 1.0 / unpack(cbuf[it, 0] + cbuf[it, 1], 0, 6)
    rowscale = 1.0 / unpack(sums, 0, 3)
    loss_ref[...] = (lse - rowscale * unpack(sums, 3, 3)).reshape(R)
    beta = weight * rowscale
    bbuf[y] = pack([beta], 4)
    send_y(bbuf, abs_.at[1], abr.at[1])

    y_chain_end()
    fill_student(y_at(4))
    wait_for(abuf.at[pl.ds(0, NY - 1)], abr.at[0])

    def scale_students(buf):
        for g in range(NY):
            factor = unpack(buf[g], 0, 3)
            scaled[:, g * R : (g + 1) * R] = (snt[g].astype(F32) * factor).astype(BF16)

    scale_students(abuf)

    def student_part(h):
        right = jnp.concatenate([pf[g, h] for g in range(NY)], axis=0)
        return jnp.dot(scaled[...], right, preferred_element_type=F32)

    def teacher_part(h):
        right = ef[h].reshape(NY * R, KB)
        return jnp.dot(scaled[...], right, preferred_element_type=F32)

    vsend[...] = student_part(o).astype(BF16)
    send_core(vsend, vrecv, vbs.at[0], vbr.at[0])
    z_chain_end()
    fill_teacher(z_at(4))
    x_chain_end()
    fill_teacher(NZ + x_at(1))
    fill_teacher(NZ + x_at(NX - 1))
    fill_teacher(NZ + x_at(2))
    vacc[...] = student_part(c)
    wait_for(bbuf.at[pl.ds(0, NY - 1)], abr.at[1])
    scale_students(bbuf)
    bsend[...] = teacher_part(o).astype(BF16)
    send_core(bsend, brecv, vbs.at[1], vbr.at[1])
    student_z(1)
    teacher = teacher_part(c)

    wait_for(vrecv, vbr.at[0])
    wait_for(brecv, vbr.at[1])
    xg = vacc[...] + vrecv[...].astype(F32) - cvec[pl.ds(y, 1), :] * (teacher + brecv[...].astype(F32))
    xg = xg.T
    floats = wraw[y].astype(F32)
    inv = lax.rsqrt(jnp.sum(floats * floats, axis=1, keepdims=True) + EPS)
    unit = floats * inv
    gp_ref[...] = ((xg - unit * jnp.sum(unit * xg, axis=1, keepdims=True)) * inv).astype(BF16)

    rows = lax.broadcasted_iota(jnp.int32, (16, R), 0)
    lanes = lax.broadcasted_iota(jnp.int32, (16, R), 1)
    pick = jnp.where((lanes == rows + pr * PR) & (rows < PR), 1.0, 0.0)
    dsn = jnp.sum(pick * alpha, axis=1, keepdims=True) * student_end(0)
    dsn = dsn - jnp.sum(pick * beta, axis=1, keepdims=True) * student_end(1)
    mine = jnp.dot(pick.astype(BF16), s_ref[...], preferred_element_type=F32)
    inv = lax.rsqrt(jnp.sum(mine * mine, axis=1, keepdims=True) + EPS)
    mine = mine * inv
    grad = (dsn - mine * jnp.sum(mine * dsn, axis=1, keepdims=True)) * inv
    gs_ref[...] = grad[:PR]

    for ref, sem in late:
        wait_for(ref, sem)


def write_outputs(loss_in, gs_in, gp_in, loss_ref, gs_ref, gp_ref):
    loss_ref[...] = loss_in[...]
    gs_ref[...] = gs_in[...]
    gp_ref[...] = gp_in[...]


def shards(teacher_feat, student_feat, prototypes, row_weight):
    vmem = pl.BlockSpec(memory_space=pltpu.VMEM)
    anywhere = pl.BlockSpec(memory_space=pl.ANY)
    dma = pltpu.SemaphoreType.DMA
    scratch = [
        pltpu.VMEM((NB, KB, D), BF16),
        pltpu.VMEM((2 * KB, D), BF16),
        pltpu.VMEM((NB, KB, D), BF16),
        pltpu.VMEM((NB, D, KB), BF16),
        pltpu.VMEM((NC, KB, D), BF16),
        pltpu.VMEM((NC, R, D), BF16),
        pltpu.VMEM((NC, R, D), BF16),
        pltpu.VMEM((PIECES, NY, PIECE, D), BF16),
        pltpu.VMEM((NY, R, D), BF16),
        pltpu.VMEM((NY, D, R), BF16),
        pltpu.VMEM((NB, NC, R, KB), BF16),
        pltpu.VMEM((NB, NC, R, KB), BF16),
        pltpu.VMEM((NB, NC, R, KB), BF16),
        pltpu.VMEM((NC, NY, PIECES, PIECE, KB), BF16),
        pltpu.VMEM((NY, NC, R, KB), BF16),
        pltpu.VMEM((2, NC, R, D), F32),
        pltpu.VMEM((D, KB), F32),
        pltpu.VMEM((D, NY * R), BF16),
        pltpu.VMEM((NB, KB), F32),
        pltpu.VMEM((ITERS, NY, NB, KB), F32),
        pltpu.VMEM((ITERS, NP, 8, 128), F32),
        pltpu.VMEM((ITERS - 1, NC, 8, 128), F32),
        pltpu.VMEM((2, 8, 128), F32),
        pltpu.VMEM((2, 4, 128), F32),
        pltpu.VMEM((NP, 4, 128), F32),
        pltpu.VMEM((NY, 4, 128), F32),
        pltpu.VMEM((NY, 4, 128), F32),
        pltpu.VMEM((2, R, D), BF16),
        pltpu.VMEM((2, R, D), BF16),
        pltpu.VMEM((2, NZ, 16, D), BF16),
        pltpu.VMEM((2, NZ, 16, D), BF16),
        pltpu.VMEM((2, NX, NZ, 16, D), BF16),
        pltpu.VMEM((2, NX, NZ, 16, D), BF16),
        pltpu.VMEM((D, KB), BF16),
        pltpu.VMEM((D, KB), BF16),
        pltpu.VMEM((D, KB), BF16),
        pltpu.VMEM((D, KB), BF16),
        dma((NB + 1,)),
        dma((2,)), dma((2,)),
        dma((ITERS,)), dma((ITERS,)),
        dma((ITERS + 1,)), dma((ITERS + 1,)),
        dma((ITERS + 1,)), dma((ITERS + 1,)),
        dma((2,)), dma((2,)),
        dma((2, 4)), dma((2, 4)),
        dma((2, 2)), dma((2, 2)),
        dma((2, 4)), dma((2, 4)),
        dma((2,)), dma((2,)),
        dma((2, 3)), dma((2, 3)),
        dma((2,)), dma((2,)),
    ]
    loss, grad_student, grad_proto = pl.pallas_call(
        kernel,
        out_shape=(
            jax.ShapeDtypeStruct((R,), F32),
            jax.ShapeDtypeStruct((PR, D), F32),
            jax.ShapeDtypeStruct((KB, D), BF16),
        ),
        in_specs=[vmem, vmem, anywhere, vmem],
        out_specs=(vmem, vmem, vmem),
        scratch_shapes=scratch,
        compiler_params=pltpu.CompilerParams(
            collective_id=0, has_side_effects=True, vmem_limit_bytes=56 * 2**20
        ),
        name="sinkhorn_head",
    )(teacher_feat, student_feat, prototypes, row_weight)
    return pl.pallas_call(
        write_outputs,
        out_shape=(
            jax.ShapeDtypeStruct((R,), F32),
            jax.ShapeDtypeStruct((PR, D), F32),
            jax.ShapeDtypeStruct((KB, D), BF16),
        ),
        in_specs=[vmem] * 3,
        out_specs=(vmem,) * 3,
        name="write_outputs",
    )(loss, grad_student, grad_proto)


def solution(mesh):
    return jax.shard_map(
        shards,
        mesh=mesh,
        in_specs=(P("dp", None), P("dp", None), P("proto", None), P("dp")),
        out_specs=(P("dp"), P(("dp", "proto"), None), P(("proto", "dp"), None)),
        check_vma=False,
    )
```

```python
import math

import jax
import jax.numpy as jnp
from jax import lax
from jax.experimental import pallas as pl
from jax.experimental.pallas import tpu as pltpu
from jax.sharding import PartitionSpec as P

MESH = pl.DeviceIdType.MESH
F32, BF16 = jnp.float32, jnp.bfloat16
ITERS = 3
NY, NC, NZ, NX = 8, 2, 8, 4
NP = NZ * NX
R = 384
D = 384
KB = 256
NB = 8
PIECE = 32
PIECES = R // PIECE
PR = R // NP
EPS = 1e-6
EXPO_SCALE = 25.0 * math.log2(math.e)
NT = (((1,), (1,)), ((), ()))


def hops(step, size):
    return min(step, size - step)


Y_STEPS = sorted(range(1, NY), key=lambda a: -hops(a, NY))
Z_STEPS = sorted(range(1, NZ), key=lambda a: -hops(a, NZ))
X_STEPS = sorted(range(1, NX), key=lambda a: -hops(a, NX))
ZX_STEPS = sorted(
    [(a, b) for a in range(NZ) for b in range(NX) if (a, b) != (0, 0)],
    key=lambda s: -(hops(s[0], NZ) + hops(s[1], NX)),
)


def unit_rows(values):
    floats = values.astype(F32)
    return floats * lax.rsqrt(jnp.sum(floats * floats, axis=-1, keepdims=True) + EPS)


def two_rows(vector):
    high = vector.astype(BF16).astype(F32)
    low = vector - high
    rows = lax.broadcasted_iota(jnp.int32, (16, vector.shape[1]), 0)
    return jnp.where(rows == 0, high, jnp.where(rows == 1, low, 0.0)).astype(BF16)


def pack(vectors, rows):
    parts = [v[:, j : j + 128] for v in vectors for j in range(0, v.shape[1], 128)]
    if len(parts) < rows:
        parts.append(jnp.zeros((rows - len(parts), 128), F32))
    return jnp.concatenate(parts, axis=0)


def unpack(tile, start, count):
    return jnp.concatenate([tile[j : j + 1, :] for j in range(start, start + count)], axis=1)


def kernel(
    t_ref, s_ref, w_ref, rw_ref, loss_ref, gs_ref, gp_ref,
    wraw, wfraw, wn, wnt, wnf, tn2, sn2, gt, gs, snt, expo, expoz, prob, ef, pf, uw,
    vacc, scaled, cvec, ybuf, zxbuf, cbuf, c3buf, auxc, auxzx, abuf, bbuf,
    ucs, ucr, uzs, uzr, uxs, uxr, vsend, vrecv, bsend, brecv,
    wsem, xs, xr, ys, yr, zxs, zxr, cs, cr, gts, gtr, tcs, tcr, hcs, hcr, scs, scr, abs_, abr,
    us, ur, vbs, vbr,
):
    dp, pr = lax.axis_index("dp"), lax.axis_index("proto")
    y, c = lax.div(dp, NC), lax.rem(dp, NC)
    z, x = lax.div(pr, NX), lax.rem(pr, NX)
    o = 1 - c

    def dev(yy, cc, zz, xx):
        return {"dp": yy * NC + cc, "proto": zz * NX + xx}

    sibling = dev(y, o, z, x)
    y_at = lambda a: lax.rem(y + a, NY)
    z_at = lambda a: lax.rem(z + a, NZ)
    x_at = lambda a: lax.rem(x + a, NX)
    late = []

    def wait_for(ref, sem):
        pltpu.make_async_copy(ref, ref, sem).wait()

    def send(src, dst, ss, rs, to):
        pltpu.make_async_remote_copy(
            src_ref=src, dst_ref=dst, send_sem=ss, recv_sem=rs, device_id=to, device_id_type=MESH
        ).start()

    def send_y(ref, ss, rs):
        for a in Y_STEPS:
            send(ref.at[y], ref.at[y], ss, rs, dev(y_at(a), c, z, x))
        late.append((ref.at[pl.ds(0, NY - 1)], ss))

    def send_zx(ref, ss, rs):
        for a, b in ZX_STEPS:
            send(ref.at[pr], ref.at[pr], ss, rs, dev(y, c, z_at(a), x_at(b)))
        late.append((ref.at[pl.ds(0, NP - 1)], ss))

    def send_core(src, dst, ss, rs):
        send(src, dst, ss, rs, sibling)
        late.append((src, ss))

    loads = [
        pltpu.make_async_copy(w_ref.at[pl.ds((2 * b + c) * KB, KB)], wraw.at[b], wsem.at[b])
        for b in range(NB)
    ]
    loads.append(pltpu.make_async_copy(w_ref.at[pl.ds(2 * y * KB, 2 * KB)], wfraw, wsem.at[NB]))
    for load in loads:
        load.start()
    barrier = pltpu.get_barrier_semaphore()
    peers = [sibling]
    peers += [dev(y, c, z_at(a), x_at(b)) for a, b in ZX_STEPS]
    peers += [dev(y_at(a), c, z, x) for a in Y_STEPS]
    for peer in peers:
        pl.semaphore_signal(barrier, inc=1, device_id=peer, device_id_type=MESH)

    tn_own = unit_rows(t_ref[...]).astype(BF16)
    tn2[c] = tn_own

    def expo_block(b, h):
        e = jnp.exp2(lax.dot_general(tn2[h], wn[b], NT, preferred_element_type=F32) * EXPO_SCALE)
        expo[b, h] = e.astype(BF16)
        return jnp.sum(e, axis=0, keepdims=True)

    for b in range(NB):
        loads[b].wait()
        wn[b] = unit_rows(wraw[b]).astype(BF16)
        ybuf[0, y, b : b + 1, :] = expo_block(b, c)
    sn_own = unit_rows(s_ref[...]).astype(BF16)
    sn2[c] = sn_own
    for b in range(NB):
        wnt[b] = wn[b].T
    loads[NB].wait()
    for h in range(NC):
        wnf[h] = unit_rows(wfraw[pl.ds(h * KB, KB), :]).astype(BF16)

    def y_chain(step):
        if step > 1:
            for way, back in ((0, -(step - 1)), (1, step - 1)):
                wait_for(gs.at[y_at(NY + back)], scr.at[way, step - 2])
        for way, back, to in ((0, -(step - 1), 1), (1, step - 1, -1)):
            src = gs.at[y_at(NY + back)]
            if step == 4:
                src = src.at[pl.ds(way * (R // 2), R // 2)]
            send(src, src, scs.at[way, step - 1], scr.at[way, step - 1], dev(y_at(NY + to), c, z, x))
            late.append((src, scs.at[way, step - 1]))

    def y_chain_end():
        for way in range(2):
            wait_for(gs.at[y_at(4), pl.ds(way * (R // 2), R // 2)], scr.at[way, 3])

    def z_chain(step):
        if step == 1:
            wait_for(gt.at[z, pl.ds(0, NY - 1)], gtr.at[0])
        else:
            for way, back in ((0, -(step - 1)), (1, step - 1)):
                wait_for(gt.at[z_at(NZ + back)], tcr.at[way, step - 2])
        for way, back, to in ((0, -(step - 1), 1), (1, step - 1, -1)):
            src = gt.at[z_at(NZ + back)]
            if step == 4:
                src = src.at[pl.ds(way * (NY // 2), NY // 2)]
            send(src, src, tcs.at[way, step - 1], tcr.at[way, step - 1], dev(y, c, z_at(NZ + to), x))
            late.append((src, tcs.at[way, step - 1]))

    def z_chain_end():
        for way in range(2):
            wait_for(gt.at[z_at(4), pl.ds(way * (NY // 2), NY // 2)], tcr.at[way, 3])

    def x_chain(step):
        if step == 1:
            wait_for(gt.at[NZ + x, pl.ds(0, NY - 1)], gtr.at[1])
        else:
            for way, back in ((0, -1), (1, 1)):
                wait_for(gt.at[NZ + x_at(NX + back)], hcr.at[way, 0])
        for way, back, to in ((0, -(step - 1), 1), (1, step - 1, -1)):
            src = gt.at[NZ + x_at(NX + back)]
            if step == 2:
                src = src.at[pl.ds(way * (NY // 2), NY // 2)]
            send(src, src, hcs.at[way, step - 1], hcr.at[way, step - 1], dev(y, c, z, x_at(NX + to)))
            late.append((src, hcs.at[way, step - 1]))

    def x_chain_end():
        for way in range(2):
            wait_for(gt.at[NZ + x_at(2), pl.ds(way * (NY // 2), NY // 2)], hcr.at[way, 1])

    pl.semaphore_wait(barrier, len(peers))
    send_core(tn2.at[c], tn2.at[c], xs.at[0], xr.at[0])
    gs[y] = sn_own
    send_core(sn2.at[c], sn2.at[c], xs.at[1], xr.at[1])
    y_chain(1)

    def spread_teacher(i):
        piece = (z, NZ + x)[i]
        gt[piece, y] = tn2[c, pl.ds(pl.multiple_of(piece * PIECE, PIECE), PIECE), :]
        for a in Y_STEPS:
            send(gt.at[piece, y], gt.at[piece, y], gts.at[i], gtr.at[i], dev(y_at(a), c, z, x))
        late.append((gt.at[0, pl.ds(0, NY - 1)], gts.at[i]))

    def student_block(b, h):
        zs = lax.dot_general(sn2[h], wn[b], NT, preferred_element_type=F32) * 10.0
        prob[b, h] = jnp.exp(zs).astype(BF16)
        expoz[b, h] = (expo[b, h].astype(F32) * zs).astype(BF16)

    for b in range(NB // 2):
        student_block(b, c)
    wait_for(tn2.at[o], xr.at[0])
    for b in range(NB):
        ybuf[0, y, b : b + 1, :] += expo_block(b, o)

    def fill_teacher(piece):
        rows = gt[piece].reshape(NY * PIECE, D)
        for h in range(NC):
            st = lax.dot_general(rows, wnf[h], NT, preferred_element_type=F32)
            e = jnp.exp2(st * EXPO_SCALE).astype(BF16)
            for g in range(NY):
                ef[h, g, piece] = e[g * PIECE : (g + 1) * PIECE]

    def fill_student(group):
        rows = gs[group]
        snt[group] = rows.T
        for h in range(NC):
            zs = lax.dot_general(rows, wnf[h], NT, preferred_element_type=F32) * 10.0
            pf[group, h] = jnp.exp(zs).astype(BF16)

    def own(v):
        return jnp.where(c == 0, v[:, :R], v[:, R:])

    def other(v):
        return jnp.where(c == 0, v[:, R:], v[:, :R])

    def row_sums(mat, scale, matmuls):
        total = jnp.zeros((16, NC * R), F32)
        lanes = jnp.zeros((NC * R, 128), F32)
        for b in range(NB):
            block = mat[b].reshape(NC * R, KB)
            if b < matmuls:
                total = total + lax.dot_general(
                    two_rows(scale[b : b + 1, :]), block, NT, preferred_element_type=F32
                )
            else:
                block = block.astype(F32)
                if scale is not None:
                    block = block * scale[b : b + 1, :]
                lanes = lanes + (block[:, :128] + block[:, 128:])
        vector = jnp.sum(lanes.T, axis=0, keepdims=True)
        return vector + total[0:1] + total[1:2] if matmuls else vector

    def sum_protos(q, mat, scale):
        def half(h, carry):
            left = jnp.concatenate([mat[b, h] for b in range(NB)], axis=1)
            if scale is None:
                right = jnp.concatenate([wnt[b] for b in range(NB)], axis=1)
            else:
                right = jnp.concatenate(
                    [(wnt[b].astype(F32) * scale[b : b + 1, :]).astype(BF16) for b in range(NB)], axis=1
                )
            uw[q, h] = lax.dot_general(left, right, NT, preferred_element_type=F32)
            return carry

        lax.fori_loop(0, NC, half, 0)
        ucs[q] = uw[q, o].astype(BF16)
        send_core(ucs.at[q], ucr.at[q], us.at[q, 0], ur.at[q, 0])

    def student_x(q):
        wait_for(ucr.at[q], ur.at[q, 0])
        total = uw[q, c] + ucr[q].astype(F32)
        pad = jnp.zeros((16 - PR, D), F32)
        for i in range(NP):
            tile = jnp.concatenate([total[i * PR : (i + 1) * PR], pad], axis=0)
            uxs[q, i % NX, i // NX] = tile.astype(BF16)
        uxr[q, x] = uxs[q, x]
        for a in X_STEPS:
            send(uxs.at[q, x_at(a)], uxr.at[q, x], us.at[q, 1], ur.at[q, 1], dev(y, c, z, x_at(a)))
        late.append((uxs.at[q, pl.ds(0, NX - 1)], us.at[q, 1]))

    def student_z(q):
        wait_for(uxr.at[q, pl.ds(0, NX - 1)], ur.at[q, 1])
        uzs[q] = jnp.sum(uxr[q].astype(F32), axis=0).astype(BF16)
        uzr[q, z] = uzs[q, z]
        for a in Z_STEPS:
            send(uzs.at[q, z_at(a)], uzr.at[q, z], us.at[q, 2], ur.at[q, 2], dev(y, c, z_at(a), x))
        late.append((uzs.at[q, pl.ds(0, NZ - 1)], us.at[q, 2]))

    def student_end(q):
        wait_for(uzr.at[q, pl.ds(0, NZ - 1)], ur.at[q, 2])
        return jnp.sum(uzr[q].astype(F32), axis=0)

    rowscale = None
    for it in range(ITERS):
        last = it == ITERS - 1
        if it > 0:
            left = two_rows(rowscale)
            for b in range(NB):
                both = jnp.dot(left, expo[b].reshape(NC * R, KB), preferred_element_type=F32)
                ybuf[it, y, b : b + 1, :] = both[0:1] + both[1:2]
        send_y(ybuf.at[it], ys.at[it], yr.at[it])
        if it == 0:
            for b in range(NB // 2, NB):
                student_block(b, c)
            wait_for(sn2.at[o], xr.at[1])
            for b in range(NB):
                student_block(b, o)
        elif it == 1:
            z_chain(2)
            wait_for(auxc.at[1], cr.at[ITERS])
            auxzx[pr] = pack([expsum_own], 4) + auxc[1]
            send_zx(auxzx, zxs.at[ITERS], zxr.at[ITERS])
            fill_teacher(z)
            fill_student(y_at(1))
            fill_student(y_at(NY - 1))
        else:
            wait_for(auxzx.at[pl.ds(0, NP - 1)], zxr.at[ITERS])
            expsum = unpack(jnp.sum(auxzx[...], axis=0), 0, 3)
            lse = jnp.log(expsum)
            weight = rw_ref[...].reshape(1, R) * 10.0
            alpha = weight / expsum
            abuf[y] = pack([alpha], 4)
            send_y(abuf, abs_.at[0], abr.at[0])
            student_z(0)
            fill_student(y_at(2))
            fill_student(y_at(NY - 2))
            fill_teacher(z_at(2))
            fill_teacher(z_at(NZ - 2))
            fill_teacher(NZ + x)
        wait_for(ybuf.at[it, pl.ds(0, NY - 1)], yr.at[it])
        if it < 2:
            spread_teacher(it)
        if it > 0:
            y_chain(it + 2)
        if last:
            z_chain(4)
            x_chain(2)
        colscale = 1.0 / jnp.sum(ybuf[it], axis=0)
        cvec[...] = colscale
        if not last:
            tot = row_sums(expo, colscale, 3)
            zxbuf[it, pr] = pack([tot], 8)
        else:
            tot = row_sums(expo, colscale, 3)
            qz = row_sums(expoz, colscale, 3)
            c3buf[0] = pack([other(tot), other(qz)], 8)
            send_core(c3buf.at[0], c3buf.at[1], cs.at[it], cr.at[it])
            mine = pack([own(tot), own(qz)], 8)
            wait_for(c3buf.at[1], cr.at[it])
            zxbuf[it, pr] = mine + c3buf[1]
        send_zx(zxbuf.at[it], zxs.at[it], zxr.at[it])
        if it == 0:
            expsum = row_sums(prob, None, 0)
            auxc[0] = pack([other(expsum)], 4)
            send_core(auxc.at[0], auxc.at[1], cs.at[ITERS], cr.at[ITERS])
            expsum_own = own(expsum)
            y_chain(2)
            sum_protos(0, prob, None)
            fill_student(y)
            z_chain(1)
        elif it == 1:
            student_x(0)
            fill_teacher(z_at(1))
            fill_teacher(z_at(NZ - 1))
        else:
            sum_protos(1, expo, colscale)
            fill_student(y_at(3))
            fill_student(y_at(NY - 3))
            student_x(1)
            fill_teacher(z_at(3))
            fill_teacher(z_at(NZ - 3))
        wait_for(zxbuf.at[it, pl.ds(0, NP - 1)], zxr.at[it])
        sums = jnp.sum(zxbuf[it], axis=0)
        if not last:
            cbuf[it, c] = sums
            send_core(cbuf.at[it, c], cbuf.at[it, c], cs.at[it], cr.at[it])
            if it == 1:
                z_chain(3)
                x_chain(1)
            wait_for(cbuf.at[it, o], cr.at[it])
            rowscale = 1.0 / unpack(cbuf[it, 0] + cbuf[it, 1], 0, 6)
    rowscale = 1.0 / unpack(sums, 0, 3)
    loss_ref[...] = (lse - rowscale * unpack(sums, 3, 3)).reshape(R)
    beta = weight * rowscale
    bbuf[y] = pack([beta], 4)
    send_y(bbuf, abs_.at[1], abr.at[1])

    y_chain_end()
    fill_student(y_at(4))
    wait_for(abuf.at[pl.ds(0, NY - 1)], abr.at[0])

    def scale_students(buf):
        for g in range(NY):
            factor = unpack(buf[g], 0, 3)
            scaled[:, g * R : (g + 1) * R] = (snt[g].astype(F32) * factor).astype(BF16)

    scale_students(abuf)

    def student_part(h):
        right = jnp.concatenate([pf[g, h] for g in range(NY)], axis=0)
        return jnp.dot(scaled[...], right, preferred_element_type=F32)

    def teacher_part(h):
        right = ef[h].reshape(NY * R, KB)
        return jnp.dot(scaled[...], right, preferred_element_type=F32)

    vsend[...] = student_part(o).astype(BF16)
    send_core(vsend, vrecv, vbs.at[0], vbr.at[0])
    z_chain_end()
    fill_teacher(z_at(4))
    x_chain_end()
    fill_teacher(NZ + x_at(1))
    fill_teacher(NZ + x_at(NX - 1))
    fill_teacher(NZ + x_at(2))
    vacc[...] = student_part(c)
    wait_for(bbuf.at[pl.ds(0, NY - 1)], abr.at[1])
    scale_students(bbuf)
    bsend[...] = teacher_part(o).astype(BF16)
    send_core(bsend, brecv, vbs.at[1], vbr.at[1])
    student_z(1)
    teacher = teacher_part(c)

    wait_for(vrecv, vbr.at[0])
    wait_for(brecv, vbr.at[1])
    xg = vacc[...] + vrecv[...].astype(F32) - cvec[pl.ds(y, 1), :] * (teacher + brecv[...].astype(F32))
    xg = xg.T
    floats = wraw[y].astype(F32)
    inv = lax.rsqrt(jnp.sum(floats * floats, axis=1, keepdims=True) + EPS)
    unit = floats * inv
    gp_ref[...] = ((xg - unit * jnp.sum(unit * xg, axis=1, keepdims=True)) * inv).astype(BF16)

    rows = lax.broadcasted_iota(jnp.int32, (16, R), 0)
    lanes = lax.broadcasted_iota(jnp.int32, (16, R), 1)
    pick = jnp.where((lanes == rows + pr * PR) & (rows < PR), 1.0, 0.0)
    dsn = jnp.sum(pick * alpha, axis=1, keepdims=True) * student_end(0)
    dsn = dsn - jnp.sum(pick * beta, axis=1, keepdims=True) * student_end(1)
    mine = jnp.dot(pick.astype(BF16), s_ref[...], preferred_element_type=F32)
    inv = lax.rsqrt(jnp.sum(mine * mine, axis=1, keepdims=True) + EPS)
    mine = mine * inv
    grad = (dsn - mine * jnp.sum(mine * dsn, axis=1, keepdims=True)) * inv
    gs_ref[...] = grad[:PR]

    for ref, sem in late:
        wait_for(ref, sem)


def write_outputs(loss_in, gs_in, gp_in, loss_ref, gs_ref, gp_ref):
    loss_ref[...] = loss_in[...]
    gs_ref[...] = gs_in[...]
    gp_ref[...] = gp_in[...]


def shards(teacher_feat, student_feat, prototypes, row_weight):
    vmem = pl.BlockSpec(memory_space=pltpu.VMEM)
    anywhere = pl.BlockSpec(memory_space=pl.ANY)
    dma = pltpu.SemaphoreType.DMA
    scratch = [
        pltpu.VMEM((NB, KB, D), BF16),
        pltpu.VMEM((2 * KB, D), BF16),
        pltpu.VMEM((NB, KB, D), BF16),
        pltpu.VMEM((NB, D, KB), BF16),
        pltpu.VMEM((NC, KB, D), BF16),
        pltpu.VMEM((NC, R, D), BF16),
        pltpu.VMEM((NC, R, D), BF16),
        pltpu.VMEM((PIECES, NY, PIECE, D), BF16),
        pltpu.VMEM((NY, R, D), BF16),
        pltpu.VMEM((NY, D, R), BF16),
        pltpu.VMEM((NB, NC, R, KB), BF16),
        pltpu.VMEM((NB, NC, R, KB), BF16),
        pltpu.VMEM((NB, NC, R, KB), BF16),
        pltpu.VMEM((NC, NY, PIECES, PIECE, KB), BF16),
        pltpu.VMEM((NY, NC, R, KB), BF16),
        pltpu.VMEM((2, NC, R, D), F32),
        pltpu.VMEM((D, KB), F32),
        pltpu.VMEM((D, NY * R), BF16),
        pltpu.VMEM((NB, KB), F32),
        pltpu.VMEM((ITERS, NY, NB, KB), F32),
        pltpu.VMEM((ITERS, NP, 8, 128), F32),
        pltpu.VMEM((ITERS - 1, NC, 8, 128), F32),
        pltpu.VMEM((2, 8, 128), F32),
        pltpu.VMEM((2, 4, 128), F32),
        pltpu.VMEM((NP, 4, 128), F32),
        pltpu.VMEM((NY, 4, 128), F32),
        pltpu.VMEM((NY, 4, 128), F32),
        pltpu.VMEM((2, R, D), BF16),
        pltpu.VMEM((2, R, D), BF16),
        pltpu.VMEM((2, NZ, 16, D), BF16),
        pltpu.VMEM((2, NZ, 16, D), BF16),
        pltpu.VMEM((2, NX, NZ, 16, D), BF16),
        pltpu.VMEM((2, NX, NZ, 16, D), BF16),
        pltpu.VMEM((D, KB), BF16),
        pltpu.VMEM((D, KB), BF16),
        pltpu.VMEM((D, KB), BF16),
        pltpu.VMEM((D, KB), BF16),
        dma((NB + 1,)),
        dma((2,)), dma((2,)),
        dma((ITERS,)), dma((ITERS,)),
        dma((ITERS + 1,)), dma((ITERS + 1,)),
        dma((ITERS + 1,)), dma((ITERS + 1,)),
        dma((2,)), dma((2,)),
        dma((2, 4)), dma((2, 4)),
        dma((2, 2)), dma((2, 2)),
        dma((2, 4)), dma((2, 4)),
        dma((2,)), dma((2,)),
        dma((2, 3)), dma((2, 3)),
        dma((2,)), dma((2,)),
    ]
    loss, grad_student, grad_proto = pl.pallas_call(
        kernel,
        out_shape=(
            jax.ShapeDtypeStruct((R,), F32),
            jax.ShapeDtypeStruct((PR, D), F32),
            jax.ShapeDtypeStruct((KB, D), BF16),
        ),
        in_specs=[vmem, vmem, anywhere, vmem],
        out_specs=(vmem, vmem, vmem),
        scratch_shapes=scratch,
        compiler_params=pltpu.CompilerParams(
            collective_id=0, has_side_effects=True, vmem_limit_bytes=56 * 2**20
        ),
        name="sinkhorn_head",
    )(teacher_feat, student_feat, prototypes, row_weight)
    return pl.pallas_call(
        write_outputs,
        out_shape=(
            jax.ShapeDtypeStruct((R,), F32),
            jax.ShapeDtypeStruct((PR, D), F32),
            jax.ShapeDtypeStruct((KB, D), BF16),
        ),
        in_specs=[vmem] * 3,
        out_specs=(vmem,) * 3,
        name="write_outputs",
    )(loss, grad_student, grad_proto)


def solution(mesh):
    return jax.shard_map(
        shards,
        mesh=mesh,
        in_specs=(P("dp", None), P("dp", None), P("proto", None), P("dp")),
        out_specs=(P("dp"), P(("dp", "proto"), None), P(("proto", "dp"), None)),
        check_vma=False,
    )
```
